128 devices in a mesh: img: 32 (over z, y, core), tp: 4 (over x).
Axes of the slice: x: 4, y: 4, z: 4, core: 2. Of those that a mesh axis runs over, the one named last changes fastest.
Arguments:
- tokens: bfloat16 [128, 256, 1024], P('img', 'tp'), may hold values from -6 to 6
- image_pairs: int32 [128, 2], replicated, may hold values from 0 to 127, as said below
- image_row: int32 [128], replicated, may hold values from 0 to 127, as said below
- embed_weight: bfloat16 [1024, 768], replicated, may hold values from -0.1875 to 0.1875
- norm_gain: float32 [2, 4, 768], replicated, may hold values from 0.5 to 1.5
- norm_bias: float32 [2, 4, 768], replicated, may hold values from -2 to 2
- self_qkv: bfloat16 [2, 3, 768, 768], P(None, None, None, 'tp'), may hold values from -0.21875 to 0.21875
- self_out: bfloat16 [2, 768, 768], P(None, 'tp'), may hold values from -0.21875 to 0.21875
- cross_qkv: bfloat16 [2, 3, 768, 768], P(None, None, None, 'tp'), may hold values from -0.21875 to 0.21875
- cross_out: bfloat16 [2, 768, 768], P(None, 'tp'), may hold values from -0.21875 to 0.21875
- mlp_up: bfloat16 [2, 768, 3072], P(None, None, 'tp'), may hold values from -0.21875 to 0.21875
- mlp_down: bfloat16 [2, 3072, 768], P(None, 'tp'), may hold values from -0.109375 to 0.109375
Outputs:
- features: bfloat16 [128, 256, 768], P('img', 'tp')
The draws below stay inside these ranges and needn't reach their ends.
Inputs may be any that keep to these rules, and one draw needn't show every extreme that they name: `image_pairs`: the two images of a pair differ. For each worker w, of the 8 images of pairs w * 4 to (w + 1) * 4 - 1, at most 1 have rows in one owner's block (rows o * 4 to (o + 1) * 4 - 1), and for every worker some owner's block holds exactly 1 of them; an image may appear more than once. `image_row`: A permutation of the rows.
All inputs are finite; a program needn't handle non-finite values.
Results may differ from the reference program's by a relative error of at most 0.014.
Values may be sent and summed in bfloat16 or wider, within the bound.
A program may use at most 128 MiB of HBM per device.

```python
import jax
import jax.numpy as jnp
from jax import lax

D = 768
E = 1024
FF = 3072
HEADS = 12
HEAD = 64
L = 256
PAIR_DEV = 4
IMG_DEV = 4
PAIRS = 128
IMAGES = 128
CAP = 1
N_IMG = 32
N_TP = 4


def layout(key):
    image_row = jax.random.permutation(jax.random.fold_in(key, 101), IMAGES).astype(jnp.int32)
    views = 2 * PAIR_DEV
    base = jnp.tile(jnp.arange(CAP * N_IMG, dtype=jnp.int32)[None, :], (N_IMG, 1))
    shuffled = jax.random.permutation(jax.random.fold_in(key, 102), base, axis=1, independent=True)
    owners = (shuffled[:, :views] // CAP).reshape(N_IMG, PAIR_DEV, 2)
    local_index = jax.random.randint(jax.random.fold_in(key, 103), (N_IMG, PAIR_DEV, 2), 0, IMG_DEV).astype(jnp.int32)
    step_on = jax.random.randint(jax.random.fold_in(key, 104), (N_IMG, PAIR_DEV), 1, IMG_DEV).astype(jnp.int32)
    other = jnp.where(owners[..., 0] == owners[..., 1], (local_index[..., 0] + step_on) % IMG_DEV, local_index[..., 1])
    rows = owners * IMG_DEV + jnp.stack([local_index[..., 0], other], axis=-1)
    image_of_row = jnp.zeros((IMAGES,), jnp.int32).at[image_row].set(jnp.arange(IMAGES, dtype=jnp.int32))
    image_pairs = image_of_row[rows.reshape(PAIRS, 2)]
    return (image_pairs, image_row)


def draw_image_pairs(key, part):
    image_pairs, image_row = layout(key)
    return image_pairs


def draw_image_row(key, part):
    image_pairs, image_row = layout(key)
    return image_row


def levels(stream_key, dims, split, smallest, high):
    def one(dim, shards_of):
        heights = jax.random.uniform(jax.random.fold_in(jax.random.fold_in(stream_key, 6), dim), (shards_of,), jnp.float32, smallest / len(split), high / len(split))
        return jnp.repeat(jnp.exp(heights), dims[dim] // shards_of).reshape((-1,) + (1,) * (len(dims) - dim - 1))

    level = one(*split[0])
    for cut in split[1:]:
        level = level * one(*cut)
    return level


def normal_values(rng, dims, scale, limit, pieces=(), held_as=jnp.bfloat16):
    level = levels(rng, dims, pieces, -0.22, 0.18) if pieces else 1.0
    entries = jax.random.normal(rng, dims, jnp.float32) * scale * level
    return jnp.minimum(jnp.maximum(entries, -limit), limit).astype(held_as)


def setup_inputs(seed: int = 0) -> dict:
    streams_of = jax.random.split(jax.random.key(seed), 13)
    tokens = normal_values(streams_of[0], (IMAGES, L, E), 1.0, 6.0, ((0, 32), (1, 4)))
    image_pairs = draw_image_pairs(jax.random.fold_in(streams_of[12], 71), 0)
    image_row = draw_image_row(jax.random.fold_in(streams_of[12], 71), 0)
    embed_weight = normal_values(streams_of[3], (E, D), E ** -0.5, 0.1875)
    norm_gain = jnp.clip(1.0 + 0.1 * jax.random.normal(streams_of[4], (2, 4, D), jnp.float32), 0.5, 1.5)
    norm_bias = normal_values(streams_of[5], (2, 4, D), 0.3, 2.0, (), jnp.float32)
    self_qkv = normal_values(streams_of[6], (2, 3, D, D), D ** -0.5, 0.21875, ((3, 4),))
    self_out = normal_values(streams_of[7], (2, D, D), D ** -0.5, 0.21875, ((1, 4),))
    cross_qkv = normal_values(streams_of[8], (2, 3, D, D), D ** -0.5, 0.21875, ((3, 4),))
    cross_out = normal_values(streams_of[9], (2, D, D), D ** -0.5, 0.21875, ((1, 4),))
    mlp_up = normal_values(streams_of[10], (2, D, FF), D ** -0.5, 0.21875, ((2, 4),))
    mlp_down = normal_values(streams_of[11], (2, FF, D), FF ** -0.5, 0.109375, ((1, 4),))
    return dict(tokens=tokens, image_pairs=image_pairs, image_row=image_row, embed_weight=embed_weight, norm_gain=norm_gain, norm_bias=norm_bias, self_qkv=self_qkv, self_out=self_out, cross_qkv=cross_qkv, cross_out=cross_out, mlp_up=mlp_up, mlp_down=mlp_down)


eps = 1e-06

def layer_norm(value, gain, shift):
    mean = lax.optimization_barrier(jnp.mean(value, axis=-1, keepdims=True))
    centred = value - mean
    spread = lax.optimization_barrier(jnp.mean(centred * centred, axis=-1, keepdims=True))
    return centred * lax.rsqrt(spread + eps) * gain + shift

def linear(rows, weight):
    return jnp.dot(rows, weight, preferred_element_type=jnp.float32)

def attend(query, keys, values):
    length = query.shape[0]
    q_heads = query.astype(jnp.float32).reshape(length, HEADS, HEAD)
    k_heads = keys.astype(jnp.float32).reshape(keys.shape[0], HEADS, HEAD)
    v_heads = values.astype(jnp.float32).reshape(values.shape[0], HEADS, HEAD)
    scores = jnp.einsum('qhd,khd->hqk', q_heads, k_heads) * HEAD ** (-0.5)
    weights = jax.nn.softmax(scores, axis=-1).astype(jnp.bfloat16).astype(jnp.float32)
    mixed = jnp.einsum('hqk,khd->qhd', weights, v_heads)
    return mixed.reshape(length, D).astype(jnp.bfloat16)

def grouped(mixed, weight):
    length = mixed.shape[0]
    parts = jnp.einsum('lgx,gxd->gld', mixed.astype(jnp.float32).reshape(length, N_TP, -1), weight.astype(jnp.float32).reshape(N_TP, -1, weight.shape[1]))
    return lax.optimization_barrier(jnp.sum(parts.astype(jnp.bfloat16).astype(jnp.float32), axis=0))

def decode(side, own, partner, norm_gain, norm_bias, self_qkv, self_out, cross_qkv, cross_out, mlp_up, mlp_down):

    def normed(value, which):
        return layer_norm(value, norm_gain[side, which], norm_bias[side, which]).astype(jnp.bfloat16)
    state = own.astype(jnp.float32)
    held = normed(state, 0)
    query = linear(held, self_qkv[side, 0]).astype(jnp.bfloat16)
    keys = linear(held, self_qkv[side, 1]).astype(jnp.bfloat16)
    values = linear(held, self_qkv[side, 2]).astype(jnp.bfloat16)
    state = state + grouped(attend(query, keys, values), self_out[side])
    held = normed(state, 1)
    other = normed(partner.astype(jnp.float32), 2)
    query = linear(held, cross_qkv[side, 0]).astype(jnp.bfloat16)
    keys = linear(other, cross_qkv[side, 1]).astype(jnp.bfloat16)
    values = linear(other, cross_qkv[side, 2]).astype(jnp.bfloat16)
    state = state + grouped(attend(query, keys, values), cross_out[side])
    held = normed(state, 3)
    hidden = jax.nn.gelu(linear(held, mlp_up[side]), approximate=False).astype(jnp.bfloat16)
    return state + grouped(hidden, mlp_down[side])

def reference(tokens, image_pairs, image_row, embed_weight, norm_gain, norm_bias, self_qkv, self_out, cross_qkv, cross_out, mlp_up, mlp_down):

    def one_pair(pair):
        rows = image_row[pair].astype(jnp.int32)
        first = linear(tokens[rows[0]], embed_weight).astype(jnp.bfloat16)
        second = linear(tokens[rows[1]], embed_weight).astype(jnp.bfloat16)
        weights = (norm_gain, norm_bias, self_qkv, self_out, cross_qkv, cross_out, mlp_up, mlp_down)
        out_first = decode(0, first, second, *weights)
        out_second = decode(1, second, first, *weights)
        return (jnp.stack([out_first, out_second]), rows)
    decoded, rows = lax.map(one_pair, image_pairs)
    total = jnp.zeros((IMAGES, L, D), jnp.float32)
    total = total.at[rows.reshape(-1)].add(decoded.reshape(-1, L, D))
    return total.astype(jnp.bfloat16)
```

```python
import jax
import jax.numpy as jnp
from jax import lax
from jax.experimental import pallas as pl
from jax.experimental.pallas import tpu as pltpu
from jax.sharding import PartitionSpec as P

D = 768
HEAD = 64
ROWS = 64
IMG = 32
TP = 4
VIEWS = 8
EPS = 1e-06
MESH = pl.DeviceIdType.MESH

WEIGHTS = ((768, 1152), (192, 768), (192, 768), (768, 768), (768, 768))


def layer_norm(value, gain, shift):
    mean = jnp.mean(value, axis=-1, keepdims=True)
    centred = value - mean
    spread = jnp.mean(centred * centred, axis=-1, keepdims=True)
    return (centred * lax.rsqrt(spread + EPS) * gain + shift).astype(jnp.bfloat16)


def dot(a, b):
    return jnp.dot(a, b, preferred_element_type=jnp.float32)


def attend(q, k, v):
    scores = lax.dot_general(q, k, (((1,), (1,)), ((), ())), preferred_element_type=jnp.float32)
    scores = scores * HEAD**-0.5
    top = jnp.max(scores, axis=-1, keepdims=True)
    weights = jnp.exp(scores - top)
    total = jnp.sum(weights, axis=-1, keepdims=True)
    return (dot(weights.astype(jnp.bfloat16), v) / total).astype(jnp.bfloat16)


def kernel(
    index_ref,
    tokens_ref,
    embed_ref,
    gain_ref,
    bias_ref,
    attn_ref,
    self_out_ref,
    cross_out_ref,
    up_ref,
    down_ref,
    out_ref,
    w_attn,
    w_so,
    w_co,
    w_up,
    w_down,
    embedded,
    send_in,
    recv_in,
    pair_send,
    pair_recv,
    state,
    normed,
    partner,
    mixed,
    unit_send,
    unit_recv,
    send_out,
    recv_out,
    own_sem,
    ring_send,
    ring_recv,
    a2a_send,
    a2a_recv,
    pair_sems,
):
    me = lax.axis_index("img")
    t = lax.axis_index("tp")
    core = lax.rem(me, 2)
    side = lax.rem(me // 8, 2)
    base = me - 8 * side
    sibling = me + 1 - 2 * core
    right = lax.rem(t + 1, TP)
    left = lax.rem(t + 3, TP)
    across = lax.rem(t + 2, TP)

    barrier = pltpu.get_barrier_semaphore()

    def greet_plane(step, carry):
        pl.semaphore_signal(
            barrier, inc=1, device_id=(lax.rem(me + step, IMG), t), device_id_type=MESH
        )
        return carry

    lax.fori_loop(1, IMG, greet_plane, 0)
    for unit in range(2):
        for step in range(1, TP):
            pl.semaphore_signal(
                barrier,
                inc=1,
                device_id=(base + 8 * unit, lax.rem(t + step, TP)),
                device_id_type=MESH,
            )
    pl.semaphore_wait(barrier, IMG - 1 + 2 * (TP - 1))

    sources = (
        attn_ref,
        self_out_ref.at[side],
        cross_out_ref.at[side],
        up_ref.at[side],
        down_ref.at[side],
    )
    held = (w_attn, w_so, w_co, w_up, w_down)

    def local(i):
        return pltpu.make_async_copy(sources[i], held[i].at[t], own_sem.at[i])

    def piece(i, kind):
        rows = WEIGHTS[i][0]
        half, part = rows // 2, rows // 4
        begin = core * half
        here = held[i]
        if kind == 0:
            src, dst, to = sources[i].at[pl.ds(begin, half)], here.at[t, pl.ds(begin, half)], (me, right)
        elif kind == 1:
            src, dst, to = sources[i].at[pl.ds(begin, half)], here.at[t, pl.ds(begin, half)], (me, left)
        elif kind == 2:
            src = dst = here.at[left, pl.ds(begin, part)]
            to = (me, right)
        elif kind == 3:
            src = dst = here.at[right, pl.ds(begin + part, part)]
            to = (me, left)
        elif kind == 4:
            src = dst = here.at[left, pl.ds(begin, half)]
            to = (sibling, t)
        elif kind == 5:
            src = dst = here.at[right, pl.ds(begin, half)]
            to = (sibling, t)
        else:
            src = dst = here.at[across, pl.ds(begin, half)]
            to = (sibling, t)
        return pltpu.make_async_remote_copy(
            src_ref=src,
            dst_ref=dst,
            send_sem=ring_send.at[i, kind],
            recv_sem=ring_recv.at[i, kind],
            device_id=to,
            device_id_type=MESH,
        )

    def begin_ring(i):
        piece(i, 0).start()
        piece(i, 1).start()
        local(i).start()

    def forward_ring(i):
        piece(i, 0).wait_recv()
        piece(i, 2).start()
        piece(i, 4).start()
        piece(i, 1).wait_recv()
        piece(i, 3).start()
        piece(i, 5).start()

    def share_ring(i):
        piece(i, 2).wait_recv()
        piece(i, 3).wait_recv()
        piece(i, 6).start()

    def finish_ring(i):
        local(i).wait()
        piece(i, 4).wait_recv()
        piece(i, 5).wait_recv()
        piece(i, 6).wait_recv()

    begin_ring(0)
    begin_ring(1)

    for image in range(4):
        embedded[image] = dot(tokens_ref[image], embed_ref[...]).astype(jnp.bfloat16)

    def slot_in(dest):
        return pltpu.make_async_remote_copy(
            src_ref=send_in.at[dest],
            dst_ref=recv_in.at[me],
            send_sem=a2a_send.at[0],
            recv_sem=a2a_recv.at[0],
            device_id=(dest, t),
            device_id_type=MESH,
        )

    def send_slot(step, carry):
        dest = lax.rem(me + step, IMG)
        send_in[dest] = embedded[index_ref[dest]]
        slot_in(dest).start()
        return carry

    lax.fori_loop(1, IMG, send_slot, 0)
    recv_in[me] = embedded[index_ref[me]]

    begin_ring(2)
    forward_ring(0)
    forward_ring(1)
    begin_ring(3)
    share_ring(0)
    share_ring(1)
    forward_ring(2)
    begin_ring(4)

    def whole(ref, sem):
        return pltpu.make_async_copy(ref.at[pl.ds(0, IMG - 1)], ref.at[pl.ds(0, IMG - 1)], sem)

    whole(recv_in, a2a_recv.at[0]).wait()

    for view in range(VIEWS):
        pair_send[view // 2, view % 2] = recv_in[index_ref[IMG + view]]

    def pair_copy(flip, step):
        pair = lax.rem(t + step, TP)
        to = base + 8 * (side + flip - 2 * side * flip)
        return pltpu.make_async_remote_copy(
            src_ref=pair_send.at[pair],
            dst_ref=pair_recv.at[side, t],
            send_sem=pair_sems.at[0, flip, step],
            recv_sem=pair_sems.at[1, flip, step],
            device_id=(to, pair),
            device_id_type=MESH,
        )

    others = [(flip, step) for step in range(TP) for flip in (1, 0) if flip or step]
    for flip, step in others:
        pair_copy(flip, step).start()
    pair_recv[side, t] = pair_send[t]
    share_ring(2)
    forward_ring(3)
    for flip, step in others:
        pair_copy(flip, step).wait_recv()

    for unit in range(2):
        for quarter in range(TP):
            rows = pl.ds(unit * 256 + quarter * ROWS, ROWS)
            state[rows, :] = pair_recv[unit, quarter, side].astype(jnp.float32)
            partner[rows, :] = pair_recv[unit, quarter, 1 - side]

    def norm(value, which):
        return layer_norm(value, gain_ref[side, pl.ds(which, 1)], bias_ref[side, pl.ds(which, 1)])

    for unit in range(2):
        rows = pl.ds(unit * 256, 256)
        normed[rows, :] = norm(state[rows, :], 0)
        partner[rows, :] = norm(partner[rows, :].astype(jnp.float32), 2)

    finish_ring(0)
    finish_ring(1)

    def heads(q, k, v):
        for unit in range(2):
            rows = slice(unit * 256, unit * 256 + 256)
            parts = []
            for head in range(3):
                columns = slice(head * HEAD, head * HEAD + HEAD)
                parts.append(attend(q[rows, columns], k[rows, columns], v[rows, columns]))
            mixed[rows, :] = jnp.concatenate(parts, axis=1)

    def self_group(group, carry):
        qkv = dot(normed[...], w_attn[group, :, 0:640]).astype(jnp.bfloat16)
        heads(qkv[:, 0:192], qkv[:, 192:384], qkv[:, 384:576])
        state[...] += dot(mixed[...], w_so[group])
        return carry

    lax.fori_loop(0, TP, self_group, 0)

    share_ring(3)
    forward_ring(4)
    for unit in range(2):
        rows = pl.ds(unit * 256, 256)
        normed[rows, :] = norm(state[rows, :], 1)
    finish_ring(2)

    def cross_group(group, carry):
        q = dot(normed[...], w_attn[group, :, 512:768]).astype(jnp.bfloat16)
        kv = dot(partner[...], w_attn[group, :, 768:1152]).astype(jnp.bfloat16)
        heads(q[:, 64:256], kv[:, 0:192], kv[:, 192:384])
        state[...] += dot(mixed[...], w_co[group])
        return carry

    lax.fori_loop(0, TP, cross_group, 0)

    share_ring(4)
    for unit in range(2):
        rows = pl.ds(unit * 256, 256)
        normed[rows, :] = norm(state[rows, :], 3)
    finish_ring(3)
    finish_ring(4)

    def mlp_group(group, carry):
        hidden = dot(normed[...], w_up[group])
        hidden = hidden * (lax.erf(hidden * 0.5**0.5) + 1.0) * 0.5
        state[...] += dot(hidden.astype(jnp.bfloat16), w_down[group])
        return carry

    lax.fori_loop(0, TP, mlp_group, 0)

    for unit in range(2):
        for quarter in range(TP):
            rows = pl.ds(unit * 256 + quarter * ROWS, ROWS)
            unit_send[unit, quarter] = state[rows, :].astype(jnp.bfloat16)

    def unit_copy(flip, step):
        quarter = lax.rem(t + step, TP)
        unit = side + flip - 2 * side * flip
        return pltpu.make_async_remote_copy(
            src_ref=unit_send.at[unit, quarter],
            dst_ref=unit_recv.at[t, side],
            send_sem=pair_sems.at[2, flip, step],
            recv_sem=pair_sems.at[3, flip, step],
            device_id=(base + 8 * unit, quarter),
            device_id_type=MESH,
        )

    for flip, step in others:
        unit_copy(flip, step).start()
    unit_recv[t, side] = unit_send[side, t]
    for flip, step in others:
        unit_copy(flip, step).wait_recv()

    def slot_out(dest):
        return pltpu.make_async_remote_copy(
            src_ref=send_out.at[dest],
            dst_ref=recv_out.at[me],
            send_sem=a2a_send.at[1],
            recv_sem=a2a_recv.at[1],
            device_id=(dest, t),
            device_id_type=MESH,
        )

    def send_back(step, carry):
        dest = lax.rem(me + step, IMG)
        view = index_ref[IMG + VIEWS + dest]
        send_out[dest] = unit_recv[view // 2, lax.rem(view, 2)]
        slot_out(dest).start()
        return carry

    lax.fori_loop(1, IMG, send_back, 0)
    view_here = index_ref[IMG + VIEWS + me]
    recv_out[me] = unit_recv[view_here // 2, lax.rem(view_here, 2)]

    for i in range(len(WEIGHTS)):
        for kind in range(7):
            piece(i, kind).wait_send()
    for flip, step in others:
        pair_copy(flip, step).wait_send()
        unit_copy(flip, step).wait_send()
    whole(send_in, a2a_send.at[0]).wait()
    whole(recv_out, a2a_recv.at[1]).wait()

    def add_rows(chunk, carry):
        rows = pl.ds(pl.multiple_of(chunk * 16, 16), 16)
        sums = [jnp.zeros((16, D), jnp.float32) for _ in range(4)]
        for worker in range(IMG):
            value = recv_out[worker, rows, :].astype(jnp.float32)
            image_here = index_ref[2 * IMG + VIEWS + worker]
            for image in range(4):
                sums[image] += jnp.where(image_here == image, value, 0.0)
        for image in range(4):
            out_ref[image, rows, :] = sums[image].astype(jnp.bfloat16)
        return carry

    lax.fori_loop(0, ROWS // 16, add_rows, 0)
    whole(send_out, a2a_send.at[1]).wait()


def per_device(
    tokens,
    image_pairs,
    image_row,
    embed_weight,
    norm_gain,
    norm_bias,
    self_qkv,
    self_out,
    cross_qkv,
    cross_out,
    mlp_up,
    mlp_down,
):
    me = lax.axis_index("img")
    side = lax.rem(me // 8, 2)
    img_dev = tokens.shape[0]
    rows_all = jnp.take(image_row, image_pairs.reshape(-1), axis=0).reshape(IMG, VIEWS)
    owner = rows_all // img_dev
    place = rows_all % img_dev
    from_me = owner == me
    wanted = jnp.sum(jnp.where(from_me, place, 0), axis=1)
    filled = jnp.any(from_me, axis=1)
    mine = owner[me]
    views = jnp.arange(VIEWS, dtype=jnp.int32)
    workers = jnp.arange(IMG, dtype=jnp.int32)
    back = jnp.sum(jnp.where(mine[None, :] == workers[:, None], views[None, :], 0), axis=1)
    index = jnp.concatenate([wanted, mine, back, jnp.where(filled, wanted, -1)]).astype(jnp.int32)

    qkv = jnp.concatenate(
        [
            lax.dynamic_index_in_dim(self_qkv, side, 0, keepdims=False),
            lax.dynamic_index_in_dim(cross_qkv, side, 0, keepdims=False),
        ],
        axis=0,
    )
    attn = jnp.transpose(qkv, (1, 0, 2)).reshape(D, 6 * 192)

    bf16 = jnp.bfloat16
    vmem = pl.BlockSpec(memory_space=pltpu.VMEM)
    hbm = pl.BlockSpec(memory_space=pl.ANY)
    return pl.pallas_call(
        kernel,
        out_shape=jax.ShapeDtypeStruct((img_dev, ROWS, D), bf16),
        in_specs=[pl.BlockSpec(memory_space=pltpu.SMEM)] + [vmem] * 4 + [hbm] * 5,
        out_specs=vmem,
        scratch_shapes=[pltpu.VMEM((TP,) + shape, bf16) for shape in WEIGHTS]
        + [
            pltpu.VMEM((4, ROWS, D), bf16),
            pltpu.VMEM((IMG, ROWS, D), bf16),
            pltpu.VMEM((IMG, ROWS, D), bf16),
            pltpu.VMEM((4, 2, ROWS, D), bf16),
            pltpu.VMEM((2, TP, 2, ROWS, D), bf16),
            pltpu.VMEM((512, D), jnp.float32),
            pltpu.VMEM((512, D), bf16),
            pltpu.VMEM((512, D), bf16),
            pltpu.VMEM((512, 192), bf16),
            pltpu.VMEM((2, TP, ROWS, D), bf16),
            pltpu.VMEM((4, 2, ROWS, D), bf16),
            pltpu.VMEM((IMG, ROWS, D), bf16),
            pltpu.VMEM((IMG, ROWS, D), bf16),
            pltpu.SemaphoreType.DMA((len(WEIGHTS),)),
            pltpu.SemaphoreType.DMA((len(WEIGHTS), 7)),
            pltpu.SemaphoreType.DMA((len(WEIGHTS), 7)),
            pltpu.SemaphoreType.DMA((2,)),
            pltpu.SemaphoreType.DMA((2,)),
            pltpu.SemaphoreType.DMA((4, 2, TP)),
        ],
        compiler_params=pltpu.CompilerParams(
            collective_id=0, has_side_effects=True, vmem_limit_bytes=60 * 1024 * 1024
        ),
    )(index, tokens, embed_weight, norm_gain, norm_bias, attn, self_out, cross_out, mlp_up, mlp_down)


def solution(mesh):
    in_specs = (
        P("img", "tp", None),
        P(),
        P(),
        P(),
        P(),
        P(),
        P(None, None, None, "tp"),
        P(None, "tp", None),
        P(None, None, None, "tp"),
        P(None, "tp", None),
        P(None, None, "tp"),
        P(None, "tp", None),
    )
    out_specs = P("img", "tp", None)
    return jax.shard_map(
        per_device, mesh=mesh, in_specs=in_specs, out_specs=out_specs, check_vma=False
    )
```

```python
import jax
import jax.numpy as jnp
from jax import lax
from jax.experimental import pallas as pl
from jax.experimental.pallas import tpu as pltpu
from jax.sharding import PartitionSpec as P

D = 768
HEAD = 64
ROWS = 64
IMG = 32
TP = 4
VIEWS = 8
EPS = 1e-06
MESH = pl.DeviceIdType.MESH

WEIGHTS = ((768, 1152), (192, 768), (192, 768), (768, 768), (768, 768))


ALONG = (
    (1, 1), (3, 3), (1, 3), (3, 1), (2, 2), (1, 0), (0, 1), (3, 0),
    (0, 3), (2, 1), (1, 2), (2, 3), (3, 2), (2, 0), (0, 2), (0, 0),
)
STEPS = [(z, y, c) for c in range(2) for z, y in ALONG if z or y or c]


def layer_norm(value, gain, shift):
    mean = jnp.mean(value, axis=-1, keepdims=True)
    centred = value - mean
    spread = jnp.mean(centred * centred, axis=-1, keepdims=True)
    return (centred * lax.rsqrt(spread + EPS) * gain + shift).astype(jnp.bfloat16)


def dot(a, b):
    return jnp.dot(a, b, preferred_element_type=jnp.float32)


def attend(q, k, v):
    scores = lax.dot_general(q, k, (((1,), (1,)), ((), ())), preferred_element_type=jnp.float32)
    scores = scores * HEAD**-0.5
    top = jnp.max(scores, axis=-1, keepdims=True)
    weights = jnp.exp(scores - top)
    total = jnp.sum(weights, axis=-1, keepdims=True)
    return (dot(weights.astype(jnp.bfloat16), v) / total).astype(jnp.bfloat16)


def kernel(
    index_ref,
    tokens_ref,
    embed_ref,
    gain_ref,
    bias_ref,
    attn_ref,
    self_out_ref,
    cross_out_ref,
    up_ref,
    down_ref,
    out_ref,
    w_attn,
    w_so,
    w_co,
    w_up,
    w_down,
    embedded,
    send_in,
    recv_in,
    pair_send,
    pair_recv,
    state,
    normed,
    partner,
    mixed,
    unit_send,
    unit_recv,
    send_out,
    recv_out,
    own_sem,
    ring_send,
    ring_recv,
    a2a_send,
    a2a_recv,
    pair_sems,
):
    me = lax.axis_index("img")
    t = lax.axis_index("tp")
    core = lax.rem(me, 2)
    y = lax.rem(me // 2, 4)
    z = me // 8
    side = lax.rem(z, 2)
    sibling = me + 1 - 2 * core
    right = lax.rem(t + 1, TP)
    left = lax.rem(t + 3, TP)
    across = lax.rem(t + 2, TP)

    def at(step):
        other = core + step[2] - 2 * core * step[2]
        return (lax.rem(z + step[0], 4) * 4 + lax.rem(y + step[1], 4)) * 2 + other

    giver = lax.rem(me + 24 - 16 * core, IMG)
    taker = lax.rem(me + 8 + 16 * core, IMG)

    barrier = pltpu.get_barrier_semaphore()

    def greet_plane(step, carry):
        pl.semaphore_signal(
            barrier, inc=1, device_id=(lax.rem(me + step, IMG), t), device_id_type=MESH
        )
        return carry

    lax.fori_loop(1, IMG, greet_plane, 0)
    for worker in (me, giver, taker):
        for step in range(1, TP):
            pl.semaphore_signal(
                barrier, inc=1, device_id=(worker, lax.rem(t + step, TP)), device_id_type=MESH
            )
    pl.semaphore_wait(barrier, IMG - 1 + 3 * (TP - 1))

    sources = (
        attn_ref,
        self_out_ref.at[side],
        cross_out_ref.at[side],
        up_ref.at[side],
        down_ref.at[side],
    )
    held = (w_attn, w_so, w_co, w_up, w_down)

    def local(i):
        return pltpu.make_async_copy(sources[i], held[i].at[t], own_sem.at[i])

    def split(i):
        return 2 if i < 3 else 4

    def piece(i, kind, quarter=None):
        rows = WEIGHTS[i][0]
        block = rows // split(i)
        half = block // 2
        mine = core if i < 3 else 2 * lax.rem(y, 2) + core
        theirs = core if i < 3 else 2 - 2 * lax.rem(y, 2) + core
        here = held[i]
        which = {"left": left, "right": right, "across": across}.get(quarter)
        n = ("left", "right", "across").index(quarter) if quarter else 0
        if kind == "send":
            begin, count, to = mine * block, block, (me, right if quarter == "left" else left)
            src, dst, sem = sources[i], here.at[t], n
        elif kind == "pass":
            begin = mine * block + (0 if quarter == "left" else half)
            count, to = half, (me, right if quarter == "left" else left)
            src, dst, sem = here.at[which], here.at[which], 2 + n
        elif kind == "core":
            begin, count, to = mine * block, block, (sibling, t)
            src, dst, sem = here.at[which], here.at[which], 4 + n
        elif kind == "up":
            begin, count, to = mine * block, half, (at((0, 1, 0)), t)
            src, dst, sem = here.at[which], here.at[which], 7 + n
        elif kind == "down":
            begin, count, to = mine * block + half, half, (at((0, 3, 0)), t)
            src, dst, sem = here.at[which], here.at[which], 10 + n
        else:
            begin, count, to = theirs * block, block, (sibling, t)
            src, dst, sem = here.at[which], here.at[which], 13 + n
        return pltpu.make_async_remote_copy(
            src_ref=src.at[pl.ds(begin, count)],
            dst_ref=dst.at[pl.ds(begin, count)],
            send_sem=ring_send.at[i, sem],
            recv_sem=ring_recv.at[i, sem],
            device_id=to,
            device_id_type=MESH,
        )

    def spread(i, quarter):
        for kind in ("core",) if i < 3 else ("up", "down", "core"):
            piece(i, kind, quarter).start()

    def begin_ring(i):
        piece(i, "send", "left").start()
        piece(i, "send", "right").start()
        local(i).start()

    def forward_ring(i):
        for quarter in ("left", "right"):
            piece(i, "send", quarter).wait_recv()
            piece(i, "pass", quarter).start()
            spread(i, quarter)

    def share_ring(i):
        piece(i, "pass", "left").wait_recv()
        piece(i, "pass", "right").wait_recv()
        spread(i, "across")

    def swap_ring(i, quarter):
        piece(i, "up", quarter).wait_recv()
        piece(i, "down", quarter).wait_recv()
        piece(i, "swap", quarter).start()

    def finish_ring(i):
        local(i).wait()
        for quarter in ("left", "right", "across"):
            piece(i, "core", quarter).wait_recv()
            if i >= 3:
                piece(i, "swap", quarter).wait_recv()

    def drain_ring(i):
        for quarter in ("left", "right", "across"):
            if quarter != "across":
                piece(i, "send", quarter).wait_send()
                piece(i, "pass", quarter).wait_send()
            for kind in ("core",) if i < 3 else ("up", "down", "core", "swap"):
                piece(i, kind, quarter).wait_send()

    begin_ring(0)
    begin_ring(1)

    for image in range(4):
        embedded[image] = dot(tokens_ref[image], embed_ref[...]).astype(jnp.bfloat16)

    def slot(way, send, recv, step):
        dest = at(step)
        return pltpu.make_async_remote_copy(
            src_ref=send.at[dest],
            dst_ref=recv.at[me],
            send_sem=a2a_send.at[way],
            recv_sem=a2a_recv.at[way],
            device_id=(dest, t),
            device_id_type=MESH,
        )

    def send_slots(way, send, recv, fill):
        for step in STEPS:
            send[at(step)] = fill(at(step))
            slot(way, send, recv, step).start()
        recv[me] = fill(me)

    def whole(ref, sem):
        return pltpu.make_async_copy(ref.at[pl.ds(0, IMG - 1)], ref.at[pl.ds(0, IMG - 1)], sem)

    send_slots(0, send_in, recv_in, lambda dest: embedded[index_ref[dest]])

    forward_ring(0)
    begin_ring(2)
    forward_ring(1)
    share_ring(0)
    forward_ring(2)
    share_ring(1)

    whole(recv_in, a2a_recv.at[0]).wait()

    for view in range(VIEWS):
        pair_send[view // 2, view % 2] = recv_in[index_ref[IMG + view]]

    def pair_copy(step):
        pair = lax.rem(t + step, TP)
        return pltpu.make_async_remote_copy(
            src_ref=pair_send.at[pair],
            dst_ref=pair_recv.at[0, t],
            send_sem=pair_sems.at[0, 0, step],
            recv_sem=pair_sems.at[0, 1, step],
            device_id=(me, pair),
            device_id_type=MESH,
        )

    def pair_pass(step):
        quarter = lax.rem(t + TP - step, TP)
        return pltpu.make_async_remote_copy(
            src_ref=pair_recv.at[0, quarter],
            dst_ref=pair_recv.at[1, quarter],
            send_sem=pair_sems.at[1, 0, step],
            recv_sem=pair_sems.at[1, 1, step],
            device_id=(taker, t),
            device_id_type=MESH,
        )

    for step in (2, 1, 3):
        pair_copy(step).start()
    pair_recv[0, t] = pair_send[t]
    pair_pass(0).start()
    begin_ring(3)
    for step in (1, 3, 2):
        pair_copy(step).wait_recv()
        pair_pass(step).start()
    share_ring(2)
    begin_ring(4)
    forward_ring(3)
    for step in range(TP):
        pair_pass(step).wait_recv()

    for unit in range(2):
        for quarter in range(TP):
            rows = pl.ds(unit * 256 + quarter * ROWS, ROWS)
            state[rows, :] = pair_recv[unit, quarter, side].astype(jnp.float32)
            partner[rows, :] = pair_recv[unit, quarter, 1 - side]

    def norm(value, which):
        return layer_norm(value, gain_ref[side, pl.ds(which, 1)], bias_ref[side, pl.ds(which, 1)])

    for unit in range(2):
        rows = pl.ds(unit * 256, 256)
        normed[rows, :] = norm(state[rows, :], 0)
        partner[rows, :] = norm(partner[rows, :].astype(jnp.float32), 2)

    finish_ring(0)
    finish_ring(1)

    def heads(q, k, v):
        for unit in range(2):
            rows = slice(unit * 256, unit * 256 + 256)
            parts = []
            for head in range(3):
                columns = slice(head * HEAD, head * HEAD + HEAD)
                parts.append(attend(q[rows, columns], k[rows, columns], v[rows, columns]))
            mixed[rows, :] = jnp.concatenate(parts, axis=1)

    def self_group(group, carry):
        @pl.when(group == 1)
        def _():
            share_ring(3)

        @pl.when(group == 2)
        def _():
            forward_ring(4)
            swap_ring(3, "left")
            swap_ring(3, "right")

        qkv = dot(normed[...], w_attn[group, :, 0:640]).astype(jnp.bfloat16)
        heads(qkv[:, 0:192], qkv[:, 192:384], qkv[:, 384:576])
        state[...] += dot(mixed[...], w_so[group])
        return carry

    lax.fori_loop(0, TP, self_group, 0)

    for unit in range(2):
        rows = pl.ds(unit * 256, 256)
        normed[rows, :] = norm(state[rows, :], 1)
    finish_ring(2)

    def cross_group(group, carry):
        @pl.when(group == 0)
        def _():
            share_ring(4)
            swap_ring(3, "across")

        @pl.when(group == 2)
        def _():
            swap_ring(4, "left")
            swap_ring(4, "right")

        q = dot(normed[...], w_attn[group, :, 512:768]).astype(jnp.bfloat16)
        kv = dot(partner[...], w_attn[group, :, 768:1152]).astype(jnp.bfloat16)
        heads(q[:, 64:256], kv[:, 0:192], kv[:, 192:384])
        state[...] += dot(mixed[...], w_co[group])
        return carry

    lax.fori_loop(0, TP, cross_group, 0)

    swap_ring(4, "across")
    for unit in range(2):
        rows = pl.ds(unit * 256, 256)
        normed[rows, :] = norm(state[rows, :], 3)
    finish_ring(3)
    finish_ring(4)

    def mlp_group(group, carry):
        hidden = dot(normed[...], w_up[group])
        hidden = hidden * (lax.erf(hidden * 0.5**0.5) + 1.0) * 0.5
        state[...] += dot(hidden.astype(jnp.bfloat16), w_down[group])
        return carry

    lax.fori_loop(0, TP, mlp_group, 0)

    for unit in range(2):
        for quarter in range(TP):
            rows = pl.ds(unit * 256 + quarter * ROWS, ROWS)
            unit_send[unit, quarter] = state[rows, :].astype(jnp.bfloat16)

    def unit_copy(unit, step):
        quarter = lax.rem(t + step, TP)
        return pltpu.make_async_remote_copy(
            src_ref=unit_send.at[unit, quarter],
            dst_ref=unit_recv.at[t, side],
            send_sem=pair_sems.at[2 + unit, 0, step],
            recv_sem=pair_sems.at[2 + unit, 1, step],
            device_id=((me, giver)[unit], quarter),
            device_id_type=MESH,
        )

    others = [(unit, step) for step in (2, 1, 3, 0) for unit in (1, 0) if unit or step]
    for unit, step in others:
        unit_copy(unit, step).start()
    unit_recv[t, side] = unit_send[0, t]
    for unit, step in others:
        unit_copy(unit, step).wait_recv()

    def view_for(dest):
        view = index_ref[IMG + VIEWS + dest]
        return unit_recv[view // 2, lax.rem(view, 2)]

    send_slots(1, send_out, recv_out, view_for)

    for i in range(len(WEIGHTS)):
        drain_ring(i)
    for step in range(TP):
        if step:
            pair_copy(step).wait_send()
        pair_pass(step).wait_send()
    for unit, step in others:
        unit_copy(unit, step).wait_send()
    whole(send_in, a2a_send.at[0]).wait()
    whole(recv_out, a2a_recv.at[1]).wait()

    def add_rows(chunk, carry):
        rows = pl.ds(pl.multiple_of(chunk * 16, 16), 16)
        sums = [jnp.zeros((16, D), jnp.float32) for _ in range(4)]
        for worker in range(IMG):
            value = recv_out[worker, rows, :].astype(jnp.float32)
            image_here = index_ref[2 * IMG + VIEWS + worker]
            for image in range(4):
                sums[image] += jnp.where(image_here == image, value, 0.0)
        for image in range(4):
            out_ref[image, rows, :] = sums[image].astype(jnp.bfloat16)
        return carry

    lax.fori_loop(0, ROWS // 16, add_rows, 0)
    whole(send_out, a2a_send.at[1]).wait()


def per_device(
    tokens,
    image_pairs,
    image_row,
    embed_weight,
    norm_gain,
    norm_bias,
    self_qkv,
    self_out,
    cross_qkv,
    cross_out,
    mlp_up,
    mlp_down,
):
    me = lax.axis_index("img")
    side = lax.rem(me // 8, 2)
    img_dev = tokens.shape[0]
    rows_all = jnp.take(image_row, image_pairs.reshape(-1), axis=0).reshape(IMG, VIEWS)
    owner = rows_all // img_dev
    place = rows_all % img_dev
    from_me = owner == me
    wanted = jnp.sum(jnp.where(from_me, place, 0), axis=1)
    filled = jnp.any(from_me, axis=1)
    mine = owner[me]
    views = jnp.arange(VIEWS, dtype=jnp.int32)
    workers = jnp.arange(IMG, dtype=jnp.int32)
    back = jnp.sum(jnp.where(mine[None, :] == workers[:, None], views[None, :], 0), axis=1)
    index = jnp.concatenate([wanted, mine, back, jnp.where(filled, wanted, -1)]).astype(jnp.int32)

    qkv = jnp.concatenate(
        [
            lax.dynamic_index_in_dim(self_qkv, side, 0, keepdims=False),
            lax.dynamic_index_in_dim(cross_qkv, side, 0, keepdims=False),
        ],
        axis=0,
    )
    attn = jnp.transpose(qkv, (1, 0, 2)).reshape(D, 6 * 192)

    bf16 = jnp.bfloat16
    vmem = pl.BlockSpec(memory_space=pltpu.VMEM)
    hbm = pl.BlockSpec(memory_space=pl.ANY)
    return pl.pallas_call(
        kernel,
        out_shape=jax.ShapeDtypeStruct((img_dev, ROWS, D), bf16),
        in_specs=[pl.BlockSpec(memory_space=pltpu.SMEM)] + [vmem] * 4 + [hbm] * 5,
        out_specs=vmem,
        scratch_shapes=[pltpu.VMEM((TP,) + shape, bf16) for shape in WEIGHTS]
        + [
            pltpu.VMEM((4, ROWS, D), bf16),
            pltpu.VMEM((IMG, ROWS, D), bf16),
            pltpu.VMEM((IMG, ROWS, D), bf16),
            pltpu.VMEM((4, 2, ROWS, D), bf16),
            pltpu.VMEM((2, TP, 2, ROWS, D), bf16),
            pltpu.VMEM((512, D), jnp.float32),
            pltpu.VMEM((512, D), bf16),
            pltpu.VMEM((512, D), bf16),
            pltpu.VMEM((512, 192), bf16),
            pltpu.VMEM((2, TP, ROWS, D), bf16),
            pltpu.VMEM((4, 2, ROWS, D), bf16),
            pltpu.VMEM((IMG, ROWS, D), bf16),
            pltpu.VMEM((IMG, ROWS, D), bf16),
            pltpu.SemaphoreType.DMA((len(WEIGHTS),)),
            pltpu.SemaphoreType.DMA((len(WEIGHTS), 16)),
            pltpu.SemaphoreType.DMA((len(WEIGHTS), 16)),
            pltpu.SemaphoreType.DMA((2,)),
            pltpu.SemaphoreType.DMA((2,)),
            pltpu.SemaphoreType.DMA((4, 2, TP)),
        ],
        compiler_params=pltpu.CompilerParams(
            collective_id=0, has_side_effects=True, vmem_limit_bytes=60 * 1024 * 1024
        ),
    )(index, tokens, embed_weight, norm_gain, norm_bias, attn, self_out, cross_out, mlp_up, mlp_down)


def solution(mesh):
    in_specs = (
        P("img", "tp", None),
        P(),
        P(),
        P(),
        P(),
        P(),
        P(None, None, None, "tp"),
        P(None, "tp", None),
        P(None, None, None, "tp"),
        P(None, "tp", None),
        P(None, None, "tp"),
        P(None, "tp", None),
    )
    out_specs = P("img", "tp", None)
    return jax.shard_map(
        per_device, mesh=mesh, in_specs=in_specs, out_specs=out_specs, check_vma=False
    )
```

```python
import functools

import jax
import jax.numpy as jnp
from jax import lax
from jax.experimental import pallas as pl
from jax.experimental.pallas import tpu as pltpu
from jax.sharding import PartitionSpec as P

D = 768
HEAD = 64
ROWS = 64
PART = 32
IMG = 32
TP = 4
VIEWS = 8
EPS = 1e-06
MESH = pl.DeviceIdType.MESH

SHARE = (192, 192, 192, 192, 768, 768)
UP, DOWN = 4, 5


ALONG = (
    (1, 1), (3, 3), (1, 3), (3, 1), (2, 2), (1, 0), (0, 1), (3, 0),
    (0, 3), (2, 1), (1, 2), (2, 3), (3, 2), (2, 0), (0, 2), (0, 0),
)
STEPS = [(z, y, c) for c in range(2) for z, y in ALONG if z or y or c]


QUARTERS = ("own", "right", "left", "across")


def layer_norm(value, gain, shift):
    mean = jnp.mean(value, axis=-1, keepdims=True)
    centred = value - mean
    spread = jnp.mean(centred * centred, axis=-1, keepdims=True)
    return (centred * lax.rsqrt(spread + EPS) * gain + shift).astype(jnp.bfloat16)


def dot(a, b):
    return jnp.dot(a, b, preferred_element_type=jnp.float32)


def dot_t(a, b):
    return lax.dot_general(a, b, (((1,), (1,)), ((), ())), preferred_element_type=jnp.float32)


def attend(q, k, v):
    scores = dot_t(q, k)
    scores = scores * HEAD**-0.5
    top = jnp.max(scores, axis=-1, keepdims=True)
    weights = jnp.exp(scores - top)
    total = jnp.sum(weights, axis=-1, keepdims=True)
    return (dot(weights.astype(jnp.bfloat16), v) / total).astype(jnp.bfloat16)


def kernel(
    pairs_ref,
    row_ref,
    tokens_ref,
    embed_ref,
    gain_ref,
    bias_ref,
    self_qkv_ref,
    cross_qkv_ref,
    self_out_ref,
    cross_out_ref,
    up_ref,
    down_ref,
    out_ref,
    w_self,
    w_so,
    w_cross,
    w_co,
    w_up,
    w_down,
    embedded,
    send_in,
    recv_in_0,
    recv_in_1,
    pair_send,
    pair_recv,
    state,
    normed,
    partner,
    mixed,
    unit_send,
    unit_recv_0,
    unit_recv_1,
    send_out,
    recv_out_0,
    recv_out_1,
    wanted_ref,
    mine_ref,
    back_ref,
    own_sem,
    ring_send,
    ring_recv,
    a2a_send,
    a2a_recv,
    pair_sems,
):
    me = lax.axis_index("img")
    t = lax.axis_index("tp")
    core = lax.rem(me, 2)
    y = lax.rem(me // 2, 4)
    z = me // 8
    side = lax.rem(z, 2)
    sibling = me + 1 - 2 * core
    right = lax.rem(t + 1, TP)
    left = lax.rem(t + 3, TP)
    across = lax.rem(t + 2, TP)

    def at(step):
        other = core + step[2] - 2 * core * step[2]
        return (lax.rem(z + step[0], 4) * 4 + lax.rem(y + step[1], 4)) * 2 + other

    giver = lax.rem(me + 24 - 16 * core, IMG)
    taker = lax.rem(me + 8 + 16 * core, IMG)

    sources = (
        self_qkv_ref.at[side],
        self_out_ref.at[side],
        cross_qkv_ref.at[side],
        cross_out_ref.at[side],
        up_ref.at[side],
        down_ref.at[side],
    )
    held = (w_self, w_so, w_cross, w_co, w_up, w_down)

    def local(i):
        return pltpu.make_async_copy(sources[i], held[i].at[t], own_sem.at[i])

    for i in range(len(SHARE)):
        local(i).start()

    barrier = pltpu.get_barrier_semaphore()

    def greet_plane(step, carry):
        pl.semaphore_signal(
            barrier, inc=1, device_id=(lax.rem(me + step, IMG), t), device_id_type=MESH
        )
        return carry

    lax.fori_loop(1, IMG, greet_plane, 0)
    for worker in (me, giver, taker):
        for step in range(1, TP):
            pl.semaphore_signal(
                barrier, inc=1, device_id=(worker, lax.rem(t + step, TP)), device_id_type=MESH
            )

    def row_of(worker, view):
        return row_ref[pairs_ref[view % 2, worker * 4 + view // 2]]

    def find_wanted(worker, carry):
        found = 0
        for view in range(VIEWS):
            row = row_of(worker, view)
            found = jnp.maximum(found, jnp.where(row // 4 == me, lax.rem(row, 4) + 1, 0))
        wanted_ref[worker] = found
        return carry

    lax.fori_loop(0, IMG, find_wanted, 0)
    for view in range(VIEWS):
        mine_ref[view] = row_of(me, view) // 4

    def find_back(owner, carry):
        found = 0
        for view in range(VIEWS):
            found = jnp.maximum(found, jnp.where(mine_ref[view] == owner, view, 0))
        back_ref[owner] = found
        return carry

    lax.fori_loop(0, IMG, find_back, 0)

    for image in range(4):
        embedded[image] = dot(tokens_ref[image], embed_ref[...]).astype(jnp.bfloat16)

    pl.semaphore_wait(barrier, IMG - 1 + 3 * (TP - 1))

    def split(i):
        return 2 if i < UP else 4

    def piece(i, kind, quarter=None):
        block = SHARE[i] // split(i)
        half = block // 2
        mine = core if i < UP else 2 * lax.rem(y, 2) + core
        theirs = core if i < UP else 2 - 2 * lax.rem(y, 2) + core
        here = held[i]
        which = {"left": left, "right": right, "across": across}.get(quarter)
        n = ("left", "right", "across").index(quarter) if quarter else 0
        if kind == "send":
            begin, count, to = mine * block, block, (me, right if quarter == "left" else left)
            src, dst, sem = sources[i], here.at[t], n
        elif kind == "pass":
            begin = mine * block + (0 if quarter == "left" else half)
            count, to = half, (me, right if quarter == "left" else left)
            src, dst, sem = here.at[which], here.at[which], 2 + n
        elif kind == "core":
            begin, count, to = mine * block, block, (sibling, t)
            src, dst, sem = here.at[which], here.at[which], 4 + n
        elif kind == "up":
            begin, count, to = mine * block, half, (at((0, 1, 0)), t)
            src, dst, sem = here.at[which], here.at[which], 7 + n
        elif kind == "down":
            begin, count, to = mine * block + half, half, (at((0, 3, 0)), t)
            src, dst, sem = here.at[which], here.at[which], 10 + n
        else:
            begin, count, to = theirs * block, block, (sibling, t)
            src, dst, sem = here.at[which], here.at[which], 13 + n
        rows = pl.ds(begin, count)
        if i in (0, 2):
            rows = (slice(None), rows)
        return pltpu.make_async_remote_copy(
            src_ref=src.at[rows],
            dst_ref=dst.at[rows],
            send_sem=ring_send.at[i, sem],
            recv_sem=ring_recv.at[i, sem],
            device_id=to,
            device_id_type=MESH,
        )

    def spread(i, quarter):
        for kind in ("core",) if i < UP else ("up", "down", "core"):
            piece(i, kind, quarter).start()

    def begin_ring(i):
        piece(i, "send", "left").start()
        piece(i, "send", "right").start()

    def forward_ring(i):
        for quarter in ("left", "right"):
            piece(i, "send", quarter).wait_recv()
            piece(i, "pass", quarter).start()
            spread(i, quarter)

    def share_ring(i):
        piece(i, "pass", "left").wait_recv()
        piece(i, "pass", "right").wait_recv()
        spread(i, "across")

    def swap_ring(i, quarter):
        piece(i, "up", quarter).wait_recv()
        piece(i, "down", quarter).wait_recv()
        piece(i, "swap", quarter).start()

    def finish_ring(i, quarter):
        if quarter == "own":
            local(i).wait()
            return
        piece(i, "core", quarter).wait_recv()
        if i >= UP:
            piece(i, "swap", quarter).wait_recv()

    def drain_ring(i):
        for quarter in ("left", "right", "across"):
            if quarter != "across":
                piece(i, "send", quarter).wait_send()
                piece(i, "pass", quarter).wait_send()
            for kind in ("core",) if i < UP else ("up", "down", "core", "swap"):
                piece(i, kind, quarter).wait_send()

    begin_ring(0)
    begin_ring(1)

    recv_in = (recv_in_0, recv_in_1)
    unit_recv = (unit_recv_0, unit_recv_1)
    recv_out = (recv_out_0, recv_out_1)

    def slot(way, send, recv, step, part):
        dest = at(step)
        rows = pl.ds(part * PART, PART)
        return pltpu.make_async_remote_copy(
            src_ref=send.at[dest, rows],
            dst_ref=recv[part].at[me],
            send_sem=a2a_send.at[way, part],
            recv_sem=a2a_recv.at[way, part],
            device_id=(dest, t),
            device_id_type=MESH,
        )

    def send_slots(way, send, recv, part, fill):
        rows = pl.ds(part * PART, PART)
        for step in STEPS:
            send[at(step), rows, :] = fill(at(step), rows)
            slot(way, send, recv, step, part).start()
        recv[part][me] = fill(me, rows)

    def whole(ref, sems, way, part):
        some = ref.at[pl.ds(0, IMG - 1)]
        if ref.shape[1] == ROWS:
            some = ref.at[pl.ds(0, IMG - 1), pl.ds(part * PART, PART)]
        pltpu.make_async_copy(some, some, sems.at[way, part]).wait()

    def image_for(dest, rows):
        return embedded[jnp.maximum(wanted_ref[dest] - 1, 0), rows, :]

    send_slots(0, send_in, recv_in, 0, image_for)
    begin_ring(2)
    begin_ring(3)
    send_slots(0, send_in, recv_in, 1, image_for)
    forward_ring(0)
    forward_ring(1)

    def pair_copy(step, part):
        pair = lax.rem(t + step, TP)
        return pltpu.make_async_remote_copy(
            src_ref=pair_send.at[pair, part],
            dst_ref=pair_recv.at[0, t, part],
            send_sem=pair_sems.at[0, part, 0, step],
            recv_sem=pair_sems.at[0, part, 1, step],
            device_id=(me, pair),
            device_id_type=MESH,
        )

    def pair_pass(step, part):
        quarter = lax.rem(t + TP - step, TP)
        return pltpu.make_async_remote_copy(
            src_ref=pair_recv.at[0, quarter, part],
            dst_ref=pair_recv.at[1, quarter, part],
            send_sem=pair_sems.at[1, part, 0, step],
            recv_sem=pair_sems.at[1, part, 1, step],
            device_id=(taker, t),
            device_id_type=MESH,
        )

    def begin_pairs(part):
        whole(recv_in[part], a2a_recv, 0, part)
        for view in range(VIEWS):
            pair_send[view // 2, part, view % 2] = recv_in[part][mine_ref[view]]
        for step in (2, 1, 3):
            pair_copy(step, part).start()
        pair_recv[0, t, part] = pair_send[t, part]
        pair_pass(0, part).start()

    def pass_pairs(part):
        for step in (1, 3, 2):
            pair_copy(step, part).wait_recv()
            pair_pass(step, part).start()

    def take_unit(unit, part):
        for quarter in range(TP):
            rows = pl.ds(unit * 256 + part * 128 + quarter * PART, PART)
            state[rows, :] = pair_recv[unit, quarter, part, side].astype(jnp.float32)
            partner[rows, :] = pair_recv[unit, quarter, part, 1 - side]
        rows = pl.ds(unit * 256 + part * 128, 128)
        normed[rows, :] = norm(state[rows, :], 0)
        partner[rows, :] = norm(partner[rows, :].astype(jnp.float32), 2)

    def norm(value, which):
        return layer_norm(value, gain_ref[side, pl.ds(which, 1)], bias_ref[side, pl.ds(which, 1)])

    begin_pairs(0)
    share_ring(0)
    share_ring(1)
    forward_ring(2)
    pass_pairs(0)
    take_unit(0, 0)
    forward_ring(3)
    begin_ring(UP)
    begin_pairs(1)
    begin_ring(DOWN)
    for step in range(TP):
        pair_pass(step, 0).wait_recv()
    take_unit(1, 0)
    pass_pairs(1)
    share_ring(2)
    share_ring(3)
    take_unit(0, 1)
    forward_ring(UP)
    for step in range(TP):
        pair_pass(step, 1).wait_recv()
    take_unit(1, 1)

    for i in range(2):
        for quarter in QUARTERS:
            finish_ring(i, quarter)

    def heads(q, k, v):
        for unit in range(2):
            rows = slice(unit * 256, unit * 256 + 256)
            parts = []
            for head in range(3):
                columns = slice(head * HEAD, head * HEAD + HEAD)
                parts.append(attend(q[rows, columns], k[rows, columns], v[rows, columns]))
            mixed[rows, :] = jnp.concatenate(parts, axis=1)

    def self_group(group, carry):
        @pl.when(group == 1)
        def _():
            share_ring(UP)
            forward_ring(DOWN)

        @pl.when(group == 2)
        def _():
            swap_ring(UP, "left")
            swap_ring(UP, "right")

        @pl.when(group == 3)
        def _():
            share_ring(DOWN)
            swap_ring(UP, "across")

        qkv = dot_t(normed[...], w_self[group].reshape(576, D)).astype(jnp.bfloat16)
        heads(qkv[:, 0:192], qkv[:, 192:384], qkv[:, 384:576])
        state[...] += dot(mixed[...], w_so[group])
        return carry

    lax.fori_loop(0, TP, self_group, 0)

    for unit in range(2):
        rows = pl.ds(unit * 256, 256)
        normed[rows, :] = norm(state[rows, :], 1)
    for i in range(2, UP):
        for quarter in QUARTERS:
            finish_ring(i, quarter)

    def cross_group(group, carry):
        @pl.when(group == 0)
        def _():
            swap_ring(DOWN, "left")
            swap_ring(DOWN, "right")

        @pl.when(group == 2)
        def _():
            swap_ring(DOWN, "across")

        q = dot_t(normed[...], w_cross[group, 0]).astype(jnp.bfloat16)
        kv = dot_t(partner[...], w_cross[group, 1:3].reshape(384, D)).astype(jnp.bfloat16)
        heads(q, kv[:, 0:192], kv[:, 192:384])
        state[...] += dot(mixed[...], w_co[group])
        return carry

    lax.fori_loop(0, TP, cross_group, 0)

    for unit in range(2):
        rows = pl.ds(unit * 256, 256)
        normed[rows, :] = norm(state[rows, :], 3)

    def mlp(value, group):
        hidden = dot(value, w_up[group])
        hidden = hidden * (lax.erf(hidden * 0.5**0.5) + 1.0) * 0.5
        return dot(hidden.astype(jnp.bfloat16), w_down[group])

    finish_ring(UP, "own")
    finish_ring(DOWN, "own")

    def mlp_group(i, carry):
        @pl.when(i == 1)
        def _():
            finish_ring(UP, "right")
            finish_ring(DOWN, "right")

        @pl.when(i == 2)
        def _():
            finish_ring(UP, "left")
            finish_ring(DOWN, "left")

        state[...] += mlp(normed[...], lax.rem(t + i * (i + 1) // 2, TP))
        return carry

    lax.fori_loop(0, TP - 1, mlp_group, 0)
    finish_ring(UP, "across")
    finish_ring(DOWN, "across")

    def unit_copy(unit, step, part):
        quarter = lax.rem(t + step, TP)
        rows = pl.ds(part * PART, PART)
        return pltpu.make_async_remote_copy(
            src_ref=unit_send.at[unit, quarter, rows],
            dst_ref=unit_recv[part].at[t, side],
            send_sem=pair_sems.at[2 + unit, part, 0, step],
            recv_sem=pair_sems.at[2 + unit, part, 1, step],
            device_id=((me, giver)[unit], quarter),
            device_id_type=MESH,
        )

    others = [(unit, step) for step in (2, 1, 3, 0) for unit in (1, 0) if unit or step]

    def last_group(part, carry):
        picks = [pl.ds(pl.multiple_of(unit * 256 + part * 128, 128), 128) for unit in range(2)]
        done = mlp(jnp.concatenate([normed[rows, :] for rows in picks], axis=0), across)
        for unit in range(2):
            value = state[picks[unit], :] + done[unit * 128 : unit * 128 + 128]
            for quarter in range(TP):
                unit_send[unit, quarter, pl.ds(pl.multiple_of(part * PART, PART), PART), :] = value[
                    quarter * PART : quarter * PART + PART
                ].astype(jnp.bfloat16)
        return carry

    def begin_units(part):
        for unit, step in others:
            unit_copy(unit, step, part).start()
        rows = pl.ds(part * PART, PART)
        unit_recv[part][t, side] = unit_send[0, t, rows, :]

    def begin_return(part):
        for unit, step in others:
            unit_copy(unit, step, part).wait_recv()
        def view_for(dest, rows):
            view = back_ref[dest]
            return unit_recv[part][view // 2, lax.rem(view, 2)]

        send_slots(1, send_out, recv_out, part, view_for)

    last_group(0, 0)
    begin_units(0)
    last_group(1, 0)
    begin_units(1)
    begin_return(0)
    begin_return(1)

    for i in range(len(SHARE)):
        drain_ring(i)
    for part in range(2):
        for step in range(TP):
            if step:
                pair_copy(step, part).wait_send()
            pair_pass(step, part).wait_send()
        for unit, step in others:
            unit_copy(unit, step, part).wait_send()
        whole(send_in, a2a_send, 0, part)

    def add_rows(part, chunk, carry):
        rows = pl.ds(pl.multiple_of(chunk * 16, 16), 16)
        sums = [jnp.zeros((16, D), jnp.float32) for _ in range(4)]
        for worker in range(IMG):
            value = recv_out[part][worker, rows, :].astype(jnp.float32)
            image_here = wanted_ref[worker] - 1
            for image in range(4):
                sums[image] += jnp.where(image_here == image, value, 0.0)
        for image in range(4):
            out_ref[image, pl.ds(pl.multiple_of(part * PART + chunk * 16, 16), 16), :] = sums[image].astype(jnp.bfloat16)
        return carry

    for part in range(2):
        whole(recv_out[part], a2a_recv, 1, part)
        lax.fori_loop(0, 2, functools.partial(add_rows, part), 0)
    for part in range(2):
        whole(send_out, a2a_send, 1, part)


def per_device(
    tokens,
    image_pairs,
    image_row,
    embed_weight,
    norm_gain,
    norm_bias,
    self_qkv,
    self_out,
    cross_qkv,
    cross_out,
    mlp_up,
    mlp_down,
):
    img_dev = tokens.shape[0]
    bf16 = jnp.bfloat16
    smem = pl.BlockSpec(memory_space=pltpu.SMEM)
    vmem = pl.BlockSpec(memory_space=pltpu.VMEM)
    hbm = pl.BlockSpec(memory_space=pl.ANY)
    return pl.pallas_call(
        kernel,
        out_shape=jax.ShapeDtypeStruct((img_dev, ROWS, D), bf16),
        in_specs=[smem] * 2 + [vmem] * 4 + [hbm] * 6,
        out_specs=vmem,
        scratch_shapes=[
            pltpu.VMEM((TP, 3, SHARE[i], D) if i in (0, 2) else (TP, SHARE[i], D), bf16)
            for i in range(len(SHARE))
        ]
        + [
            pltpu.VMEM((4, ROWS, D), bf16),
            pltpu.VMEM((IMG, ROWS, D), bf16),
            pltpu.VMEM((IMG, PART, D), bf16),
            pltpu.VMEM((IMG, PART, D), bf16),
            pltpu.VMEM((4, 2, 2, PART, D), bf16),
            pltpu.VMEM((2, TP, 2, 2, PART, D), bf16),
            pltpu.VMEM((512, D), jnp.float32),
            pltpu.VMEM((512, D), bf16),
            pltpu.VMEM((512, D), bf16),
            pltpu.VMEM((512, 192), bf16),
            pltpu.VMEM((2, TP, ROWS, D), bf16),
            pltpu.VMEM((4, 2, PART, D), bf16),
            pltpu.VMEM((4, 2, PART, D), bf16),
            pltpu.VMEM((IMG, ROWS, D), bf16),
            pltpu.VMEM((IMG, PART, D), bf16),
            pltpu.VMEM((IMG, PART, D), bf16),
            pltpu.SMEM((IMG,), jnp.int32),
            pltpu.SMEM((VIEWS,), jnp.int32),
            pltpu.SMEM((IMG,), jnp.int32),
            pltpu.SemaphoreType.DMA((len(SHARE),)),
            pltpu.SemaphoreType.DMA((len(SHARE), 16)),
            pltpu.SemaphoreType.DMA((len(SHARE), 16)),
            pltpu.SemaphoreType.DMA((2, 2)),
            pltpu.SemaphoreType.DMA((2, 2)),
            pltpu.SemaphoreType.DMA((4, 2, 2, TP)),
        ],
        compiler_params=pltpu.CompilerParams(
            collective_id=0, has_side_effects=True, vmem_limit_bytes=60 * 1024 * 1024
        ),
    )(
        image_pairs.T,
        image_row,
        tokens,
        embed_weight,
        norm_gain,
        norm_bias,
        jnp.swapaxes(self_qkv, 2, 3),
        jnp.swapaxes(cross_qkv, 2, 3),
        self_out,
        cross_out,
        mlp_up,
        mlp_down,
    )


def solution(mesh):
    in_specs = (
        P("img", "tp", None),
        P(),
        P(),
        P(),
        P(),
        P(),
        P(None, None, None, "tp"),
        P(None, "tp", None),
        P(None, None, None, "tp"),
        P(None, "tp", None),
        P(None, None, "tp"),
        P(None, "tp", None),
    )
    out_specs = P("img", "tp", None)
    return jax.shard_map(
        per_device, mesh=mesh, in_specs=in_specs, out_specs=out_specs, check_vma=False
    )
```

```python
import functools

import jax
import jax.numpy as jnp
from jax import lax
from jax.experimental import pallas as pl
from jax.experimental.pallas import tpu as pltpu
from jax.sharding import PartitionSpec as P

D = 768
HEAD = 64
ROWS = 64
PART = 32
IMG = 32
TP = 4
VIEWS = 8
EPS = 1e-06
MESH = pl.DeviceIdType.MESH

SHARE = (576, 192, 576, 192, 768, 768)
SWAPPED = (2, 4, 5)
UP, DOWN = 4, 5


ALONG = (
    (1, 1), (3, 3), (1, 3), (3, 1), (2, 2), (1, 0), (0, 1), (3, 0),
    (0, 3), (2, 1), (1, 2), (2, 3), (3, 2), (2, 0), (0, 2), (0, 0),
)
STEPS = [(z, y, c) for c in range(2) for z, y in ALONG if z or y or c]


QUARTERS = ("own", "right", "left", "across")


def layer_norm(value, gain, shift):
    mean = jnp.mean(value, axis=-1, keepdims=True)
    centred = value - mean
    spread = jnp.mean(centred * centred, axis=-1, keepdims=True)
    return (centred * lax.rsqrt(spread + EPS) * gain + shift).astype(jnp.bfloat16)


def dot(a, b):
    return jnp.dot(a, b, preferred_element_type=jnp.float32)


def dot_t(a, b):
    return lax.dot_general(a, b, (((1,), (1,)), ((), ())), preferred_element_type=jnp.float32)


def attend(q, k, v):
    scores = dot_t(q, k)
    scores = scores * HEAD**-0.5
    top = jnp.max(scores, axis=-1, keepdims=True)
    weights = jnp.exp(scores - top)
    total = jnp.sum(weights, axis=-1, keepdims=True)
    return (dot(weights.astype(jnp.bfloat16), v) / total).astype(jnp.bfloat16)


def kernel(
    pairs_ref,
    row_ref,
    tokens_ref,
    embed_ref,
    gain_ref,
    bias_ref,
    self_qkv_ref,
    cross_qkv_ref,
    self_out_ref,
    cross_out_ref,
    up_ref,
    down_ref,
    out_ref,
    w_self,
    w_so,
    w_cross,
    w_co,
    w_up,
    w_down,
    embedded,
    send_in,
    recv_in_0,
    recv_in_1,
    pair_send,
    pair_recv,
    state,
    normed,
    partner,
    mixed,
    unit_send,
    unit_recv_0,
    unit_recv_1,
    send_out,
    recv_out_0,
    recv_out_1,
    wanted_ref,
    mine_ref,
    back_ref,
    own_sem,
    ring_send,
    ring_recv,
    a2a_send,
    a2a_recv,
    pair_sems,
):
    me = lax.axis_index("img")
    t = lax.axis_index("tp")
    core = lax.rem(me, 2)
    y = lax.rem(me // 2, 4)
    z = me // 8
    side = lax.rem(z, 2)
    sibling = me + 1 - 2 * core
    right = lax.rem(t + 1, TP)
    left = lax.rem(t + 3, TP)
    across = lax.rem(t + 2, TP)

    def at(step):
        other = core + step[2] - 2 * core * step[2]
        return (lax.rem(z + step[0], 4) * 4 + lax.rem(y + step[1], 4)) * 2 + other

    giver = lax.rem(me + 24 - 16 * core, IMG)
    taker = lax.rem(me + 8 + 16 * core, IMG)

    sources = (
        self_qkv_ref.at[side],
        self_out_ref.at[side],
        cross_qkv_ref.at[side],
        cross_out_ref.at[side],
        up_ref.at[side],
        down_ref.at[side],
    )
    held = (w_self, w_so, w_cross, w_co, w_up, w_down)

    def local(i):
        return pltpu.make_async_copy(sources[i], held[i].at[t], own_sem.at[i])

    for i in range(len(SHARE)):
        local(i).start()

    barrier = pltpu.get_barrier_semaphore()

    def greet_plane(step, carry):
        pl.semaphore_signal(
            barrier, inc=1, device_id=(lax.rem(me + step, IMG), t), device_id_type=MESH
        )
        return carry

    lax.fori_loop(1, IMG, greet_plane, 0)
    for worker in (me, giver, taker):
        for step in range(1, TP):
            pl.semaphore_signal(
                barrier, inc=1, device_id=(worker, lax.rem(t + step, TP)), device_id_type=MESH
            )

    def row_of(worker, view):
        return row_ref[pairs_ref[view % 2, worker * 4 + view // 2]]

    def find_wanted(worker, carry):
        found = 0
        for view in range(VIEWS):
            row = row_of(worker, view)
            found = jnp.maximum(found, jnp.where(row // 4 == me, lax.rem(row, 4) + 1, 0))
        wanted_ref[worker] = found
        return carry

    lax.fori_loop(0, IMG, find_wanted, 0)
    for view in range(VIEWS):
        mine_ref[view] = row_of(me, view) // 4

    def find_back(owner, carry):
        found = 0
        for view in range(VIEWS):
            found = jnp.maximum(found, jnp.where(mine_ref[view] == owner, view, 0))
        back_ref[owner] = found
        return carry

    lax.fori_loop(0, IMG, find_back, 0)

    for image in range(4):
        embedded[image] = dot(tokens_ref[image], embed_ref[...]).astype(jnp.bfloat16)

    pl.semaphore_wait(barrier, IMG - 1 + 3 * (TP - 1))

    def split(i):
        return 4 if i in SWAPPED else 2

    def piece(i, kind, quarter=None):
        block = SHARE[i] // split(i)
        half = (block + 31) // 32 * 16
        mine = core if i not in SWAPPED else 2 * lax.rem(y, 2) + core
        theirs = core if i not in SWAPPED else 2 - 2 * lax.rem(y, 2) + core
        here = held[i]
        which = {"left": left, "right": right, "across": across}.get(quarter)
        n = ("left", "right", "across").index(quarter) if quarter else 0
        if kind == "send":
            begin, count, to = mine * block, block, (me, right if quarter == "left" else left)
            src, dst, sem = sources[i], here.at[t], n
        elif kind == "pass":
            begin = mine * block + (0 if quarter == "left" else half)
            count = half if quarter == "left" else block - half
            to = (me, right if quarter == "left" else left)
            src, dst, sem = here.at[which], here.at[which], 2 + n
        elif kind == "core":
            begin, count, to = mine * block, block, (sibling, t)
            src, dst, sem = here.at[which], here.at[which], 4 + n
        elif kind == "up":
            begin, count, to = mine * block, half, (at((0, 1, 0)), t)
            src, dst, sem = here.at[which], here.at[which], 7 + n
        elif kind == "down":
            begin, count, to = mine * block + half, block - half, (at((0, 3, 0)), t)
            src, dst, sem = here.at[which], here.at[which], 10 + n
        else:
            begin, count, to = theirs * block, block, (sibling, t)
            src, dst, sem = here.at[which], here.at[which], 13 + n
        rows = pl.ds(begin, count)
        return pltpu.make_async_remote_copy(
            src_ref=src.at[rows],
            dst_ref=dst.at[rows],
            send_sem=ring_send.at[i, sem],
            recv_sem=ring_recv.at[i, sem],
            device_id=to,
            device_id_type=MESH,
        )

    def offer_ring(i, quarter):
        piece(i, "up", quarter).start()
        piece(i, "down", quarter).start()

    def spread(i, quarter):
        if i in (UP, DOWN):
            offer_ring(i, quarter)
        piece(i, "core", quarter).start()

    def begin_ring(i):
        piece(i, "send", "left").start()
        piece(i, "send", "right").start()

    def forward_ring(i):
        for quarter in ("left", "right"):
            piece(i, "send", quarter).wait_recv()
            piece(i, "pass", quarter).start()
            spread(i, quarter)

    def share_ring(i):
        piece(i, "pass", "left").wait_recv()
        piece(i, "pass", "right").wait_recv()
        spread(i, "across")

    def swap_ring(i, quarter):
        piece(i, "up", quarter).wait_recv()
        piece(i, "down", quarter).wait_recv()
        piece(i, "swap", quarter).start()

    def finish_ring(i, quarter):
        if quarter == "own":
            local(i).wait()
            return
        piece(i, "core", quarter).wait_recv()
        if i in SWAPPED:
            piece(i, "swap", quarter).wait_recv()

    def drain_ring(i):
        for quarter in ("left", "right", "across"):
            if quarter != "across":
                piece(i, "send", quarter).wait_send()
                piece(i, "pass", quarter).wait_send()
            for kind in ("core",) if i not in SWAPPED else ("up", "down", "core", "swap"):
                piece(i, kind, quarter).wait_send()

    begin_ring(0)
    begin_ring(1)

    recv_in = (recv_in_0, recv_in_1)
    unit_recv = (unit_recv_0, unit_recv_1)
    recv_out = (recv_out_0, recv_out_1)

    def slot(way, send, recv, step, part):
        dest = at(step)
        rows = pl.ds(part * PART, PART)
        return pltpu.make_async_remote_copy(
            src_ref=send.at[dest, rows],
            dst_ref=recv[part].at[me],
            send_sem=a2a_send.at[way, part],
            recv_sem=a2a_recv.at[way, part],
            device_id=(dest, t),
            device_id_type=MESH,
        )

    def send_slots(way, send, recv, part, fill):
        rows = pl.ds(part * PART, PART)
        for step in STEPS:
            send[at(step), rows, :] = fill(at(step), rows)
            slot(way, send, recv, step, part).start()
        recv[part][me] = fill(me, rows)

    def whole(ref, sems, way, part):
        some = ref.at[pl.ds(0, IMG - 1)]
        if ref.shape[1] == ROWS:
            some = ref.at[pl.ds(0, IMG - 1), pl.ds(part * PART, PART)]
        pltpu.make_async_copy(some, some, sems.at[way, part]).wait()

    def image_for(dest, rows):
        return embedded[jnp.maximum(wanted_ref[dest] - 1, 0), rows, :]

    send_slots(0, send_in, recv_in, 0, image_for)
    begin_ring(2)
    begin_ring(3)
    send_slots(0, send_in, recv_in, 1, image_for)
    forward_ring(0)
    forward_ring(1)

    def pair_copy(step, part):
        pair = lax.rem(t + step, TP)
        return pltpu.make_async_remote_copy(
            src_ref=pair_send.at[pair, part],
            dst_ref=pair_recv.at[0, t, part],
            send_sem=pair_sems.at[0, part, 0, step],
            recv_sem=pair_sems.at[0, part, 1, step],
            device_id=(me, pair),
            device_id_type=MESH,
        )

    def pair_pass(step, part):
        quarter = lax.rem(t + TP - step, TP)
        return pltpu.make_async_remote_copy(
            src_ref=pair_recv.at[0, quarter, part],
            dst_ref=pair_recv.at[1, quarter, part],
            send_sem=pair_sems.at[1, part, 0, step],
            recv_sem=pair_sems.at[1, part, 1, step],
            device_id=(taker, t),
            device_id_type=MESH,
        )

    def begin_pairs(part):
        whole(recv_in[part], a2a_recv, 0, part)
        for view in range(VIEWS):
            pair_send[view // 2, part, view % 2] = recv_in[part][mine_ref[view]]
        for step in (2, 1, 3):
            pair_copy(step, part).start()
        pair_recv[0, t, part] = pair_send[t, part]
        pair_pass(0, part).start()

    def pass_pairs(part):
        for step in (1, 3, 2):
            pair_copy(step, part).wait_recv()
            pair_pass(step, part).start()

    def take_unit(unit, part):
        for quarter in range(TP):
            rows = pl.ds(unit * 256 + part * 128 + quarter * PART, PART)
            state[rows, :] = pair_recv[unit, quarter, part, side].astype(jnp.float32)
            partner[rows, :] = pair_recv[unit, quarter, part, 1 - side]
        rows = pl.ds(unit * 256 + part * 128, 128)
        normed[rows, :] = norm(state[rows, :], 0)
        partner[rows, :] = norm(partner[rows, :].astype(jnp.float32), 2)

    def norm(value, which):
        return layer_norm(value, gain_ref[side, pl.ds(which, 1)], bias_ref[side, pl.ds(which, 1)])

    begin_pairs(0)
    share_ring(0)
    share_ring(1)
    forward_ring(2)
    pass_pairs(0)
    take_unit(0, 0)
    forward_ring(3)
    begin_ring(UP)
    share_ring(2)
    begin_pairs(1)
    for quarter in QUARTERS[1:]:
        offer_ring(2, quarter)
    for step in range(TP):
        pair_pass(step, 0).wait_recv()
    take_unit(1, 0)
    pass_pairs(1)
    begin_ring(DOWN)
    share_ring(3)
    take_unit(0, 1)
    forward_ring(UP)
    for step in range(TP):
        pair_pass(step, 1).wait_recv()
    take_unit(1, 1)

    for i in range(2):
        for quarter in QUARTERS:
            finish_ring(i, quarter)

    def heads(q, k, v):
        for unit in range(2):
            rows = slice(unit * 256, unit * 256 + 256)
            parts = []
            for head in range(3):
                columns = slice(head * HEAD, head * HEAD + HEAD)
                parts.append(attend(q[rows, columns], k[rows, columns], v[rows, columns]))
            mixed[rows, :] = jnp.concatenate(parts, axis=1)

    def self_group(group, carry):
        @pl.when(group == 1)
        def _():
            swap_ring(2, "right")
            swap_ring(2, "left")
            swap_ring(2, "across")

        @pl.when(group == 2)
        def _():
            share_ring(UP)
            forward_ring(DOWN)

        @pl.when(group == 3)
        def _():
            swap_ring(UP, "left")
            swap_ring(UP, "right")

        qkv = dot_t(normed[...], w_self[group]).astype(jnp.bfloat16)
        heads(qkv[:, 0:192], qkv[:, 192:384], qkv[:, 384:576])
        state[...] += dot(mixed[...], w_so[group])
        return carry

    lax.fori_loop(0, TP, self_group, 0)

    for unit in range(2):
        rows = pl.ds(unit * 256, 256)
        normed[rows, :] = norm(state[rows, :], 1)
    finish_ring(2, "own")
    finish_ring(3, "own")

    def cross_group(i, carry):
        @pl.when(i == 0)
        def _():
            share_ring(DOWN)
            swap_ring(UP, "across")

        @pl.when(i == 1)
        def _():
            swap_ring(DOWN, "left")
            swap_ring(DOWN, "right")

        @pl.when(i == 3)
        def _():
            swap_ring(DOWN, "across")

        for n in range(1, TP):

            @pl.when(i == n)
            def _():
                finish_ring(2, QUARTERS[n])
                finish_ring(3, QUARTERS[n])

        group = lax.rem(t + i * (i + 1) // 2, TP)
        q = dot_t(normed[...], w_cross[group, 0:192]).astype(jnp.bfloat16)
        kv = dot_t(partner[...], w_cross[group, 192:576]).astype(jnp.bfloat16)
        heads(q, kv[:, 0:192], kv[:, 192:384])
        state[...] += dot(mixed[...], w_co[group])
        return carry

    lax.fori_loop(0, TP, cross_group, 0)

    for unit in range(2):
        rows = pl.ds(unit * 256, 256)
        normed[rows, :] = norm(state[rows, :], 3)

    def mlp(value, group):
        hidden = dot(value, w_up[group])
        hidden = hidden * (lax.erf(hidden * 0.5**0.5) + 1.0) * 0.5
        return dot(hidden.astype(jnp.bfloat16), w_down[group])

    finish_ring(UP, "own")
    finish_ring(DOWN, "own")

    def mlp_group(i, carry):
        @pl.when(i == 1)
        def _():
            finish_ring(UP, "right")
            finish_ring(DOWN, "right")

        @pl.when(i == 2)
        def _():
            finish_ring(UP, "left")
            finish_ring(DOWN, "left")

        state[...] += mlp(normed[...], lax.rem(t + i * (i + 1) // 2, TP))
        return carry

    lax.fori_loop(0, TP - 1, mlp_group, 0)
    finish_ring(UP, "across")
    finish_ring(DOWN, "across")

    def unit_copy(unit, step, part):
        quarter = lax.rem(t + step, TP)
        rows = pl.ds(part * PART, PART)
        return pltpu.make_async_remote_copy(
            src_ref=unit_send.at[unit, quarter, rows],
            dst_ref=unit_recv[part].at[t, side],
            send_sem=pair_sems.at[2 + unit, part, 0, step],
            recv_sem=pair_sems.at[2 + unit, part, 1, step],
            device_id=((me, giver)[unit], quarter),
            device_id_type=MESH,
        )

    others = [(unit, step) for step in (2, 1, 3, 0) for unit in (1, 0) if unit or step]

    def last_group(part, carry):
        picks = [pl.ds(pl.multiple_of(unit * 256 + part * 128, 128), 128) for unit in range(2)]
        done = mlp(jnp.concatenate([normed[rows, :] for rows in picks], axis=0), across)
        for unit in range(2):
            value = state[picks[unit], :] + done[unit * 128 : unit * 128 + 128]
            for quarter in range(TP):
                unit_send[unit, quarter, pl.ds(pl.multiple_of(part * PART, PART), PART), :] = value[
                    quarter * PART : quarter * PART + PART
                ].astype(jnp.bfloat16)
        return carry

    def begin_units(part):
        for unit, step in others:
            unit_copy(unit, step, part).start()
        rows = pl.ds(part * PART, PART)
        unit_recv[part][t, side] = unit_send[0, t, rows, :]

    def begin_return(part):
        for unit, step in others:
            unit_copy(unit, step, part).wait_recv()
        def view_for(dest, rows):
            view = back_ref[dest]
            return unit_recv[part][view // 2, lax.rem(view, 2)]

        send_slots(1, send_out, recv_out, part, view_for)

    last_group(0, 0)
    begin_units(0)
    last_group(1, 0)
    begin_units(1)
    begin_return(0)
    begin_return(1)

    for i in range(len(SHARE)):
        drain_ring(i)
    for part in range(2):
        for step in range(TP):
            if step:
                pair_copy(step, part).wait_send()
            pair_pass(step, part).wait_send()
        for unit, step in others:
            unit_copy(unit, step, part).wait_send()
        whole(send_in, a2a_send, 0, part)

    def add_rows(part, chunk, carry):
        rows = pl.ds(pl.multiple_of(chunk * 16, 16), 16)
        sums = [jnp.zeros((16, D), jnp.float32) for _ in range(4)]
        for worker in range(IMG):
            value = recv_out[part][worker, rows, :].astype(jnp.float32)
            image_here = wanted_ref[worker] - 1
            for image in range(4):
                sums[image] += jnp.where(image_here == image, value, 0.0)
        for image in range(4):
            out_ref[image, pl.ds(pl.multiple_of(part * PART + chunk * 16, 16), 16), :] = sums[image].astype(jnp.bfloat16)
        return carry

    for part in range(2):
        whole(recv_out[part], a2a_recv, 1, part)
        lax.fori_loop(0, 2, functools.partial(add_rows, part), 0)
    for part in range(2):
        whole(send_out, a2a_send, 1, part)


def per_device(
    tokens,
    image_pairs,
    image_row,
    embed_weight,
    norm_gain,
    norm_bias,
    self_qkv,
    self_out,
    cross_qkv,
    cross_out,
    mlp_up,
    mlp_down,
):
    img_dev = tokens.shape[0]
    bf16 = jnp.bfloat16
    smem = pl.BlockSpec(memory_space=pltpu.SMEM)
    vmem = pl.BlockSpec(memory_space=pltpu.VMEM)
    hbm = pl.BlockSpec(memory_space=pl.ANY)
    return pl.pallas_call(
        kernel,
        out_shape=jax.ShapeDtypeStruct((img_dev, ROWS, D), bf16),
        in_specs=[smem] * 2 + [vmem] * 4 + [hbm] * 6,
        out_specs=vmem,
        scratch_shapes=[
            *(pltpu.VMEM((TP, rows, D), bf16) for rows in SHARE),
            pltpu.VMEM((4, ROWS, D), bf16),
            pltpu.VMEM((IMG, ROWS, D), bf16),
            pltpu.VMEM((IMG, PART, D), bf16),
            pltpu.VMEM((IMG, PART, D), bf16),
            pltpu.VMEM((4, 2, 2, PART, D), bf16),
            pltpu.VMEM((2, TP, 2, 2, PART, D), bf16),
            pltpu.VMEM((512, D), jnp.float32),
            pltpu.VMEM((512, D), bf16),
            pltpu.VMEM((512, D), bf16),
            pltpu.VMEM((512, 192), bf16),
            pltpu.VMEM((2, TP, ROWS, D), bf16),
            pltpu.VMEM((4, 2, PART, D), bf16),
            pltpu.VMEM((4, 2, PART, D), bf16),
            pltpu.VMEM((IMG, ROWS, D), bf16),
            pltpu.VMEM((IMG, PART, D), bf16),
            pltpu.VMEM((IMG, PART, D), bf16),
            pltpu.SMEM((IMG,), jnp.int32),
            pltpu.SMEM((VIEWS,), jnp.int32),
            pltpu.SMEM((IMG,), jnp.int32),
            pltpu.SemaphoreType.DMA((len(SHARE),)),
            pltpu.SemaphoreType.DMA((len(SHARE), 16)),
            pltpu.SemaphoreType.DMA((len(SHARE), 16)),
            pltpu.SemaphoreType.DMA((2, 2)),
            pltpu.SemaphoreType.DMA((2, 2)),
            pltpu.SemaphoreType.DMA((4, 2, 2, TP)),
        ],
        compiler_params=pltpu.CompilerParams(
            collective_id=0, has_side_effects=True, vmem_limit_bytes=60 * 1024 * 1024
        ),
    )(
        image_pairs.T,
        image_row,
        tokens,
        embed_weight,
        norm_gain,
        norm_bias,
        jnp.swapaxes(self_qkv, 2, 3).reshape(2, 576, D),
        jnp.swapaxes(cross_qkv, 2, 3).reshape(2, 576, D),
        self_out,
        cross_out,
        mlp_up,
        mlp_down,
    )


def solution(mesh):
    in_specs = (
        P("img", "tp", None),
        P(),
        P(),
        P(),
        P(),
        P(),
        P(None, None, None, "tp"),
        P(None, "tp", None),
        P(None, None, None, "tp"),
        P(None, "tp", None),
        P(None, None, "tp"),
        P(None, "tp", None),
    )
    out_specs = P("img", "tp", None)
    return jax.shard_map(
        per_device, mesh=mesh, in_specs=in_specs, out_specs=out_specs, check_vma=False
    )
```

```python
import functools
import math

import jax
import jax.numpy as jnp
from jax import lax
from jax.experimental import pallas as pl
from jax.experimental.pallas import tpu as pltpu
from jax.sharding import PartitionSpec as P

D = 768
HEAD = 64
ROWS = 64
PART = 32
IMG = 32
TP = 4
VIEWS = 8
EPS = 1e-06
MESH = pl.DeviceIdType.MESH

SHARE = (576, 192, 576, 192, 768, 768)
SWAPPED = (2, 4, 5)
UP, DOWN = 4, 5


ALONG = (
    (1, 1), (3, 3), (1, 3), (3, 1), (2, 2), (1, 0), (0, 1), (3, 0),
    (0, 3), (2, 1), (1, 2), (2, 3), (3, 2), (2, 0), (0, 2), (0, 0),
)
STEPS = [(z, y, c) for c in range(2) for z, y in ALONG if z or y or c]


QUARTERS = ("own", "right", "left", "across")


def layer_norm(value, gain, shift):
    mean = jnp.mean(value, axis=-1, keepdims=True)
    centred = value - mean
    spread = jnp.mean(centred * centred, axis=-1, keepdims=True)
    return (centred * lax.rsqrt(spread + EPS) * gain + shift).astype(jnp.bfloat16)


def dot(a, b):
    return jnp.dot(a, b, preferred_element_type=jnp.float32)


def dot_t(a, b):
    return lax.dot_general(a, b, (((1,), (1,)), ((), ())), preferred_element_type=jnp.float32)


def attend(triples):
    scores = [dot_t(q, k) for q, k, _ in triples]
    tops = [jnp.max(score, axis=-1, keepdims=True) for score in scores]
    weights = [jnp.exp2((score - top) * (HEAD**-0.5 * math.log2(math.e))) for score, top in zip(scores, tops)]
    totals = [jnp.sum(weight, axis=-1, keepdims=True) for weight in weights]
    return [
        (dot(weight.astype(jnp.bfloat16), v) / total).astype(jnp.bfloat16)
        for weight, total, (_, _, v) in zip(weights, totals, triples)
    ]


def kernel(
    pairs_ref,
    row_ref,
    tokens_ref,
    embed_ref,
    gain_ref,
    bias_ref,
    self_qkv_ref,
    cross_qkv_ref,
    self_out_ref,
    cross_out_ref,
    up_ref,
    down_ref,
    out_ref,
    w_self,
    w_so,
    w_cross,
    w_co,
    w_up,
    w_down,
    embedded,
    send_in,
    recv_in_0,
    recv_in_1,
    pair_send,
    pair_recv,
    state,
    normed,
    partner,
    mixed,
    unit_send,
    unit_recv_0,
    unit_recv_1,
    send_out,
    recv_out_0,
    recv_out_1,
    wanted_ref,
    mine_ref,
    back_ref,
    own_sem,
    ring_send,
    ring_recv,
    a2a_send,
    a2a_recv,
    pair_sems,
):
    me = lax.axis_index("img")
    t = lax.axis_index("tp")
    core = lax.rem(me, 2)
    y = lax.rem(me // 2, 4)
    z = me // 8
    side = lax.rem(z, 2)
    sibling = me + 1 - 2 * core
    right = lax.rem(t + 1, TP)
    left = lax.rem(t + 3, TP)
    across = lax.rem(t + 2, TP)

    def at(step):
        other = core + step[2] - 2 * core * step[2]
        return (lax.rem(z + step[0], 4) * 4 + lax.rem(y + step[1], 4)) * 2 + other

    giver = lax.rem(me + 24 - 16 * core, IMG)
    taker = lax.rem(me + 8 + 16 * core, IMG)

    sources = (
        self_qkv_ref.at[side],
        self_out_ref.at[side],
        cross_qkv_ref.at[side],
        cross_out_ref.at[side],
        up_ref.at[side],
        down_ref.at[side],
    )
    held = (w_self, w_so, w_cross, w_co, w_up, w_down)

    def local(i):
        return pltpu.make_async_copy(sources[i], held[i].at[t], own_sem.at[i])

    for i in range(len(SHARE)):
        local(i).start()

    barrier = pltpu.get_barrier_semaphore()

    def greet_plane(step, carry):
        pl.semaphore_signal(
            barrier, inc=1, device_id=(lax.rem(me + step, IMG), t), device_id_type=MESH
        )
        return carry

    lax.fori_loop(1, IMG, greet_plane, 0)
    for worker in (me, giver, taker):
        for step in range(1, TP):
            pl.semaphore_signal(
                barrier, inc=1, device_id=(worker, lax.rem(t + step, TP)), device_id_type=MESH
            )

    def row_of(worker, view):
        return row_ref[pairs_ref[view % 2, worker * 4 + view // 2]]

    def find_wanted(worker, carry):
        found = 0
        for view in range(VIEWS):
            row = row_of(worker, view)
            found = jnp.maximum(found, jnp.where(row >> 2 == me, (row & 3) + 1, 0))
        wanted_ref[worker] = found
        return carry

    lax.fori_loop(0, IMG, find_wanted, 0)
    for view in range(VIEWS):
        mine_ref[view] = row_of(me, view) >> 2

    def find_back(owner, carry):
        found = 0
        for view in range(VIEWS):
            found = jnp.maximum(found, jnp.where(mine_ref[view] == owner, view, 0))
        back_ref[owner] = found
        return carry

    lax.fori_loop(0, IMG, find_back, 0)

    start = dot(tokens_ref[...].reshape(4 * ROWS, tokens_ref.shape[2]), embed_ref[...])
    embedded[...] = start.astype(jnp.bfloat16).reshape(4, ROWS, D)

    pl.semaphore_wait(barrier, IMG - 1 + 3 * (TP - 1))

    def split(i):
        return 4 if i in SWAPPED else 2

    def piece(i, kind, quarter=None):
        block = SHARE[i] // split(i)
        half = (block + 31) // 32 * 16
        mine = core if i not in SWAPPED else 2 * lax.rem(y, 2) + core
        theirs = core if i not in SWAPPED else 2 - 2 * lax.rem(y, 2) + core
        here = held[i]
        which = {"left": left, "right": right, "across": across}.get(quarter)
        n = ("left", "right", "across").index(quarter) if quarter else 0
        if kind == "send":
            begin, count, to = mine * block, block, (me, right if quarter == "left" else left)
            src, dst, sem = sources[i], here.at[t], n
        elif kind == "pass":
            begin = mine * block + (0 if quarter == "left" else half)
            count = half if quarter == "left" else block - half
            to = (me, right if quarter == "left" else left)
            src, dst, sem = here.at[which], here.at[which], 2 + n
        elif kind == "core":
            begin, count, to = mine * block, block, (sibling, t)
            src, dst, sem = here.at[which], here.at[which], 4 + n
        elif kind == "up":
            begin, count, to = mine * block, half, (at((0, 1, 0)), t)
            src, dst, sem = here.at[which], here.at[which], 7 + n
        elif kind == "down":
            begin, count, to = mine * block + half, block - half, (at((0, 3, 0)), t)
            src, dst, sem = here.at[which], here.at[which], 10 + n
        else:
            begin, count, to = theirs * block, block, (sibling, t)
            src, dst, sem = here.at[which], here.at[which], 13 + n
        rows = pl.ds(begin, count)
        return pltpu.make_async_remote_copy(
            src_ref=src.at[rows],
            dst_ref=dst.at[rows],
            send_sem=ring_send.at[i, sem],
            recv_sem=ring_recv.at[i, sem],
            device_id=to,
            device_id_type=MESH,
        )

    def offer_ring(i, quarter):
        piece(i, "up", quarter).start()
        piece(i, "down", quarter).start()

    def spread(i, quarter):
        if i in (UP, DOWN):
            offer_ring(i, quarter)
        piece(i, "core", quarter).start()

    def begin_ring(i):
        piece(i, "send", "left").start()
        piece(i, "send", "right").start()

    def forward_ring(i):
        for quarter in ("left", "right"):
            piece(i, "send", quarter).wait_recv()
            piece(i, "pass", quarter).start()
            spread(i, quarter)

    def share_ring(i):
        piece(i, "pass", "left").wait_recv()
        piece(i, "pass", "right").wait_recv()
        spread(i, "across")

    def swap_ring(i, quarter):
        piece(i, "up", quarter).wait_recv()
        piece(i, "down", quarter).wait_recv()
        piece(i, "swap", quarter).start()

    def finish_ring(i, quarter):
        if quarter == "own":
            local(i).wait()
            return
        piece(i, "core", quarter).wait_recv()
        if i in SWAPPED:
            piece(i, "swap", quarter).wait_recv()

    def drain_ring(i):
        for quarter in ("left", "right", "across"):
            if quarter != "across":
                piece(i, "send", quarter).wait_send()
                piece(i, "pass", quarter).wait_send()
            for kind in ("core",) if i not in SWAPPED else ("up", "down", "core", "swap"):
                piece(i, kind, quarter).wait_send()

    begin_ring(0)
    begin_ring(1)

    recv_in = (recv_in_0, recv_in_1)
    unit_recv = (unit_recv_0, unit_recv_1)
    recv_out = (recv_out_0, recv_out_1)

    def slot(way, send, recv, step, part):
        dest = at(step)
        rows = pl.ds(part * PART, PART)
        return pltpu.make_async_remote_copy(
            src_ref=send.at[dest, rows],
            dst_ref=recv[part].at[me],
            send_sem=a2a_send.at[way, part],
            recv_sem=a2a_recv.at[way, part],
            device_id=(dest, t),
            device_id_type=MESH,
        )

    def send_slots(way, send, recv, part, fill):
        rows = pl.ds(part * PART, PART)
        for step in STEPS:
            send[at(step), rows, :] = fill(at(step), rows)
            slot(way, send, recv, step, part).start()
        recv[part][me] = fill(me, rows)

    def whole(ref, sems, way, part):
        some = ref.at[pl.ds(0, IMG - 1)]
        if ref.shape[1] == ROWS:
            some = ref.at[pl.ds(0, IMG - 1), pl.ds(part * PART, PART)]
        pltpu.make_async_copy(some, some, sems.at[way, part]).wait()

    def image_for(dest, rows):
        return embedded[jnp.maximum(wanted_ref[dest] - 1, 0), rows, :]

    send_slots(0, send_in, recv_in, 0, image_for)
    begin_ring(2)
    begin_ring(3)
    send_slots(0, send_in, recv_in, 1, image_for)
    forward_ring(0)
    forward_ring(1)

    def pair_copy(step, part):
        pair = lax.rem(t + step, TP)
        return pltpu.make_async_remote_copy(
            src_ref=pair_send.at[pair, part],
            dst_ref=pair_recv.at[0, t, part],
            send_sem=pair_sems.at[0, part, 0, step],
            recv_sem=pair_sems.at[0, part, 1, step],
            device_id=(me, pair),
            device_id_type=MESH,
        )

    def pair_pass(step, part):
        quarter = lax.rem(t + TP - step, TP)
        return pltpu.make_async_remote_copy(
            src_ref=pair_recv.at[0, quarter, part],
            dst_ref=pair_recv.at[1, quarter, part],
            send_sem=pair_sems.at[1, part, 0, step],
            recv_sem=pair_sems.at[1, part, 1, step],
            device_id=(taker, t),
            device_id_type=MESH,
        )

    def begin_pairs(part):
        whole(recv_in[part], a2a_recv, 0, part)
        for view in range(VIEWS):
            pair_send[view // 2, part, view % 2] = recv_in[part][mine_ref[view]]
        for step in (2, 1, 3):
            pair_copy(step, part).start()
        pair_recv[0, t, part] = pair_send[t, part]
        pair_pass(0, part).start()

    def pass_pairs(part):
        for step in (1, 3, 2):
            pair_copy(step, part).wait_recv()
            pair_pass(step, part).start()

    def take_unit(unit, part):
        for quarter in range(TP):
            rows = pl.ds(unit * 256 + part * 128 + quarter * PART, PART)
            state[rows, :] = pair_recv[unit, quarter, part, side].astype(jnp.float32)
            partner[rows, :] = pair_recv[unit, quarter, part, 1 - side]
        rows = pl.ds(unit * 256 + part * 128, 128)
        normed[rows, :] = norm(state[rows, :], 0)
        partner[rows, :] = norm(partner[rows, :].astype(jnp.float32), 2)

    def norm(value, which):
        return layer_norm(value, gain_ref[side, pl.ds(which, 1)], bias_ref[side, pl.ds(which, 1)])

    begin_pairs(0)
    share_ring(0)
    share_ring(1)
    forward_ring(2)
    pass_pairs(0)
    take_unit(0, 0)
    forward_ring(3)
    begin_ring(UP)
    share_ring(2)
    begin_pairs(1)
    for quarter in QUARTERS[1:]:
        offer_ring(2, quarter)
    for step in range(TP):
        pair_pass(step, 0).wait_recv()
    take_unit(1, 0)
    begin_ring(DOWN)
    pass_pairs(1)
    share_ring(3)
    take_unit(0, 1)
    forward_ring(UP)
    for step in range(TP):
        pair_pass(step, 1).wait_recv()
    take_unit(1, 1)

    for i in range(2):
        for quarter in QUARTERS:
            finish_ring(i, quarter)

    def heads(q, k, v):
        def cut(value, unit, head):
            return value[unit * 256 : unit * 256 + 256, head * HEAD : head * HEAD + HEAD]

        found = attend([[cut(x, unit, head) for x in (q, k, v)] for unit in range(2) for head in range(3)])
        for unit in range(2):
            mixed[unit * 256 : unit * 256 + 256, :] = jnp.concatenate(found[3 * unit : 3 * unit + 3], axis=1)

    def self_group(group, carry):
        @pl.when(group == 1)
        def _():
            swap_ring(2, "right")
            swap_ring(2, "left")
            swap_ring(2, "across")

        @pl.when(group == 2)
        def _():
            share_ring(UP)
            forward_ring(DOWN)

        @pl.when(group == 3)
        def _():
            swap_ring(UP, "left")
            swap_ring(UP, "right")

        qkv = dot_t(normed[...], w_self[group]).astype(jnp.bfloat16)
        heads(qkv[:, 0:192], qkv[:, 192:384], qkv[:, 384:576])
        state[...] += dot(mixed[...], w_so[group])
        return carry

    lax.fori_loop(0, TP, self_group, 0)

    for unit in range(2):
        rows = pl.ds(unit * 256, 256)
        normed[rows, :] = norm(state[rows, :], 1)
    finish_ring(2, "own")
    finish_ring(3, "own")

    def cross_group(i, carry):
        @pl.when(i == 0)
        def _():
            share_ring(DOWN)

        @pl.when(i == 2)
        def _():
            swap_ring(UP, "across")

        @pl.when(i == 3)
        def _():
            swap_ring(DOWN, "right")
            swap_ring(DOWN, "left")

        for n in range(1, TP):

            @pl.when(i == n)
            def _():
                finish_ring(2, QUARTERS[n])
                finish_ring(3, QUARTERS[n])

        group = lax.rem(t + i * (i + 1) // 2, TP)
        q = dot_t(normed[...], w_cross[group, 0:192]).astype(jnp.bfloat16)
        kv = dot_t(partner[...], w_cross[group, 192:576]).astype(jnp.bfloat16)
        heads(q, kv[:, 0:192], kv[:, 192:384])
        state[...] += dot(mixed[...], w_co[group])
        return carry

    lax.fori_loop(0, TP, cross_group, 0)

    for unit in range(2):
        rows = pl.ds(unit * 256, 256)
        normed[rows, :] = norm(state[rows, :], 3)

    def mlp(value, group):
        hidden = dot(value, w_up[group])
        hidden = hidden * (lax.erf(hidden * 0.5**0.5) + 1.0) * 0.5
        return dot(hidden.astype(jnp.bfloat16), w_down[group])

    finish_ring(UP, "own")
    finish_ring(DOWN, "own")

    def mlp_group(i, carry):
        @pl.when(i == 1)
        def _():
            swap_ring(DOWN, "across")
            finish_ring(UP, "right")
            finish_ring(DOWN, "right")

        @pl.when(i == 2)
        def _():
            finish_ring(UP, "left")
            finish_ring(DOWN, "left")

        state[...] += mlp(normed[...], lax.rem(t + i * (i + 1) // 2, TP))
        return carry

    lax.fori_loop(0, TP - 1, mlp_group, 0)
    finish_ring(UP, "across")
    finish_ring(DOWN, "across")

    def unit_copy(unit, step, part):
        quarter = lax.rem(t + step, TP)
        rows = pl.ds(part * PART, PART)
        return pltpu.make_async_remote_copy(
            src_ref=unit_send.at[unit, quarter, rows],
            dst_ref=unit_recv[part].at[t, side],
            send_sem=pair_sems.at[2 + unit, part, 0, step],
            recv_sem=pair_sems.at[2 + unit, part, 1, step],
            device_id=((me, giver)[unit], quarter),
            device_id_type=MESH,
        )

    others = [(unit, step) for step in (2, 1, 3, 0) for unit in (1, 0) if unit or step]

    def last_group(part, carry):
        picks = [pl.ds(pl.multiple_of(unit * 256 + part * 128, 128), 128) for unit in range(2)]
        done = mlp(jnp.concatenate([normed[rows, :] for rows in picks], axis=0), across)
        for unit in range(2):
            value = state[picks[unit], :] + done[unit * 128 : unit * 128 + 128]
            for quarter in range(TP):
                unit_send[unit, quarter, pl.ds(pl.multiple_of(part * PART, PART), PART), :] = value[
                    quarter * PART : quarter * PART + PART
                ].astype(jnp.bfloat16)
        return carry

    def begin_units(part):
        for unit, step in others:
            unit_copy(unit, step, part).start()
        rows = pl.ds(part * PART, PART)
        unit_recv[part][t, side] = unit_send[0, t, rows, :]

    def begin_return(part):
        for unit, step in others:
            unit_copy(unit, step, part).wait_recv()
        def view_for(dest, rows):
            view = back_ref[dest]
            return unit_recv[part][view // 2, lax.rem(view, 2)]

        send_slots(1, send_out, recv_out, part, view_for)

    last_group(0, 0)
    begin_units(0)
    last_group(1, 0)
    begin_units(1)
    begin_return(0)
    begin_return(1)

    for i in range(len(SHARE)):
        drain_ring(i)
    for part in range(2):
        for step in range(TP):
            if step:
                pair_copy(step, part).wait_send()
            pair_pass(step, part).wait_send()
        for unit, step in others:
            unit_copy(unit, step, part).wait_send()
        whole(send_in, a2a_send, 0, part)

    def add_rows(part, chunk, carry):
        rows = pl.ds(pl.multiple_of(chunk * 16, 16), 16)
        sums = [jnp.zeros((16, D), jnp.float32) for _ in range(4)]
        for worker in range(IMG):
            value = recv_out[part][worker, rows, :].astype(jnp.float32)
            image_here = wanted_ref[worker] - 1
            for image in range(4):
                sums[image] += jnp.where(image_here == image, value, 0.0)
        for image in range(4):
            out_ref[image, pl.ds(pl.multiple_of(part * PART + chunk * 16, 16), 16), :] = sums[image].astype(jnp.bfloat16)
        return carry

    for part in range(2):
        whole(recv_out[part], a2a_recv, 1, part)
        lax.fori_loop(0, 2, functools.partial(add_rows, part), 0)
    for part in range(2):
        whole(send_out, a2a_send, 1, part)


def per_device(
    tokens,
    image_pairs,
    image_row,
    embed_weight,
    norm_gain,
    norm_bias,
    self_qkv,
    self_out,
    cross_qkv,
    cross_out,
    mlp_up,
    mlp_down,
):
    img_dev = tokens.shape[0]
    bf16 = jnp.bfloat16
    smem = pl.BlockSpec(memory_space=pltpu.SMEM)
    vmem = pl.BlockSpec(memory_space=pltpu.VMEM)
    hbm = pl.BlockSpec(memory_space=pl.ANY)
    return pl.pallas_call(
        kernel,
        out_shape=jax.ShapeDtypeStruct((img_dev, ROWS, D), bf16),
        in_specs=[smem] * 2 + [vmem] * 4 + [hbm] * 6,
        out_specs=vmem,
        scratch_shapes=[
            *(pltpu.VMEM((TP, rows, D), bf16) for rows in SHARE),
            pltpu.VMEM((4, ROWS, D), bf16),
            pltpu.VMEM((IMG, ROWS, D), bf16),
            pltpu.VMEM((IMG, PART, D), bf16),
            pltpu.VMEM((IMG, PART, D), bf16),
            pltpu.VMEM((4, 2, 2, PART, D), bf16),
            pltpu.VMEM((2, TP, 2, 2, PART, D), bf16),
            pltpu.VMEM((512, D), jnp.float32),
            pltpu.VMEM((512, D), bf16),
            pltpu.VMEM((512, D), bf16),
            pltpu.VMEM((512, 192), bf16),
            pltpu.VMEM((2, TP, ROWS, D), bf16),
            pltpu.VMEM((4, 2, PART, D), bf16),
            pltpu.VMEM((4, 2, PART, D), bf16),
            pltpu.VMEM((IMG, ROWS, D), bf16),
            pltpu.VMEM((IMG, PART, D), bf16),
            pltpu.VMEM((IMG, PART, D), bf16),
            pltpu.SMEM((IMG,), jnp.int32),
            pltpu.SMEM((VIEWS,), jnp.int32),
            pltpu.SMEM((IMG,), jnp.int32),
            pltpu.SemaphoreType.DMA((len(SHARE),)),
            pltpu.SemaphoreType.DMA((len(SHARE), 16)),
            pltpu.SemaphoreType.DMA((len(SHARE), 16)),
            pltpu.SemaphoreType.DMA((2, 2)),
            pltpu.SemaphoreType.DMA((2, 2)),
            pltpu.SemaphoreType.DMA((4, 2, 2, TP)),
        ],
        compiler_params=pltpu.CompilerParams(
            collective_id=0, has_side_effects=True, vmem_limit_bytes=60 * 1024 * 1024
        ),
    )(
        image_pairs.T,
        image_row,
        tokens,
        embed_weight,
        norm_gain,
        norm_bias,
        jnp.swapaxes(self_qkv, 2, 3).reshape(2, 576, D),
        jnp.swapaxes(cross_qkv, 2, 3).reshape(2, 576, D),
        self_out,
        cross_out,
        mlp_up,
        mlp_down,
    )


def solution(mesh):
    in_specs = (
        P("img", "tp", None),
        P(),
        P(),
        P(),
        P(),
        P(),
        P(None, None, None, "tp"),
        P(None, "tp", None),
        P(None, None, None, "tp"),
        P(None, "tp", None),
        P(None, None, "tp"),
        P(None, "tp", None),
    )
    out_specs = P("img", "tp", None)
    return jax.shard_map(
        per_device, mesh=mesh, in_specs=in_specs, out_specs=out_specs, check_vma=False
    )
```

```python
import functools
import math

import jax
import jax.numpy as jnp
from jax import lax
from jax.experimental import pallas as pl
from jax.experimental.pallas import tpu as pltpu
from jax.sharding import PartitionSpec as P

D = 768
HEAD = 64
ROWS = 64
PART = 32
IMG = 32
TP = 4
VIEWS = 8
EPS = 1e-06
MESH = pl.DeviceIdType.MESH

SHARE = (576, 192, 576, 192, 768, 768)
SWAPPED = (2, 4, 5)
UP, DOWN = 4, 5


ALONG = (
    (1, 1), (3, 3), (1, 3), (3, 1), (2, 2), (1, 0), (0, 1), (3, 0),
    (0, 3), (2, 1), (1, 2), (2, 3), (3, 2), (2, 0), (0, 2), (0, 0),
)
STEPS = [(z, y, c) for c in range(2) for z, y in ALONG if z or y or c]


QUARTERS = ("own", "right", "left", "across")


def layer_norm(value, gain, shift):
    mean = jnp.mean(value, axis=-1, keepdims=True)
    centred = value - mean
    spread = jnp.mean(centred * centred, axis=-1, keepdims=True)
    return (centred * lax.rsqrt(spread + EPS) * gain + shift).astype(jnp.bfloat16)


def dot(a, b):
    return jnp.dot(a, b, preferred_element_type=jnp.float32)


def dot_t(a, b):
    return lax.dot_general(a, b, (((1,), (1,)), ((), ())), preferred_element_type=jnp.float32)


def attend(triples):
    scores = [dot_t(q, k) for q, k, _ in triples]
    tops = [jnp.max(score, axis=-1, keepdims=True) for score in scores]
    weights = [jnp.exp2((score - top) * (HEAD**-0.5 * math.log2(math.e))) for score, top in zip(scores, tops)]
    totals = [jnp.sum(weight, axis=-1, keepdims=True) for weight in weights]
    return [
        (dot(weight.astype(jnp.bfloat16), v) / total).astype(jnp.bfloat16)
        for weight, total, (_, _, v) in zip(weights, totals, triples)
    ]


def kernel(
    pairs_ref,
    row_ref,
    tokens_ref,
    embed_ref,
    gain_ref,
    bias_ref,
    self_qkv_ref,
    cross_qkv_ref,
    self_out_ref,
    cross_out_ref,
    up_ref,
    down_ref,
    out_ref,
    w_self,
    w_so,
    w_cross,
    w_co,
    w_up,
    w_down,
    embedded,
    send_in,
    recv_in_0,
    recv_in_1,
    pair_send,
    pair_recv,
    state,
    normed,
    partner,
    unit_send,
    unit_recv_0,
    unit_recv_1,
    send_out,
    recv_out_0,
    recv_out_1,
    wanted_ref,
    mine_ref,
    back_ref,
    own_sem,
    ring_send,
    ring_recv,
    a2a_send,
    a2a_recv,
    pair_sems,
):
    me = lax.axis_index("img")
    t = lax.axis_index("tp")
    core = lax.rem(me, 2)
    y = lax.rem(me // 2, 4)
    z = me // 8
    side = lax.rem(z, 2)
    sibling = me + 1 - 2 * core
    right = lax.rem(t + 1, TP)
    left = lax.rem(t + 3, TP)
    across = lax.rem(t + 2, TP)

    def at(step):
        other = core + step[2] - 2 * core * step[2]
        return (lax.rem(z + step[0], 4) * 4 + lax.rem(y + step[1], 4)) * 2 + other

    giver = lax.rem(me + 24 - 16 * core, IMG)
    taker = lax.rem(me + 8 + 16 * core, IMG)

    sources = (
        self_qkv_ref.at[side],
        self_out_ref.at[side],
        cross_qkv_ref.at[side],
        cross_out_ref.at[side],
        up_ref.at[side],
        down_ref.at[side],
    )
    held = (w_self, w_so, w_cross, w_co, w_up, w_down)

    def local(i):
        return pltpu.make_async_copy(sources[i], held[i].at[t], own_sem.at[i])

    for i in range(len(SHARE)):
        local(i).start()

    barrier = pltpu.get_barrier_semaphore()

    def greet_plane(step, carry):
        pl.semaphore_signal(
            barrier, inc=1, device_id=(lax.rem(me + step, IMG), t), device_id_type=MESH
        )
        return carry

    lax.fori_loop(1, IMG, greet_plane, 0)
    for worker in (me, giver, taker):
        for step in range(1, TP):
            pl.semaphore_signal(
                barrier, inc=1, device_id=(worker, lax.rem(t + step, TP)), device_id_type=MESH
            )

    def row_of(worker, view):
        return row_ref[pairs_ref[view % 2, worker * 4 + view // 2]]

    def find_wanted(worker, carry):
        found = 0
        for view in range(VIEWS):
            row = row_of(worker, view)
            found = jnp.maximum(found, jnp.where(row >> 2 == me, (row & 3) + 1, 0))
        wanted_ref[worker] = found
        return carry

    lax.fori_loop(0, IMG, find_wanted, 0)
    for view in range(VIEWS):
        mine_ref[view] = row_of(me, view) >> 2

    def find_back(owner, carry):
        found = 0
        for view in range(VIEWS):
            found = jnp.maximum(found, jnp.where(mine_ref[view] == owner, view, 0))
        back_ref[owner] = found
        return carry

    lax.fori_loop(0, IMG, find_back, 0)

    start = dot(tokens_ref[...].reshape(4 * ROWS, tokens_ref.shape[2]), embed_ref[...])
    embedded[...] = start.astype(jnp.bfloat16).reshape(4, ROWS, D)

    pl.semaphore_wait(barrier, IMG - 1 + 3 * (TP - 1))

    def split(i):
        return 4 if i in SWAPPED else 2

    def piece(i, kind, quarter=None):
        block = SHARE[i] // split(i)
        half = (block + 31) // 32 * 16
        mine = core if i not in SWAPPED else 2 * lax.rem(y, 2) + core
        theirs = core if i not in SWAPPED else 2 - 2 * lax.rem(y, 2) + core
        here = held[i]
        which = {"left": left, "right": right, "across": across}.get(quarter)
        n = ("left", "right", "across").index(quarter) if quarter else 0
        if kind == "send":
            begin, count, to = mine * block, block, (me, right if quarter == "left" else left)
            src, dst, sem = sources[i], here.at[t], n
        elif kind == "pass":
            begin = mine * block + (0 if quarter == "left" else half)
            count = half if quarter == "left" else block - half
            to = (me, right if quarter == "left" else left)
            src, dst, sem = here.at[which], here.at[which], 2 + n
        elif kind == "core":
            begin, count, to = mine * block, block, (sibling, t)
            src, dst, sem = here.at[which], here.at[which], 4 + n
        elif kind == "up":
            begin, count, to = mine * block, half, (at((0, 1, 0)), t)
            src, dst, sem = here.at[which], here.at[which], 7 + n
        elif kind == "down":
            begin, count, to = mine * block + half, block - half, (at((0, 3, 0)), t)
            src, dst, sem = here.at[which], here.at[which], 10 + n
        else:
            begin, count, to = theirs * block, block, (sibling, t)
            src, dst, sem = here.at[which], here.at[which], 13 + n
        rows = pl.ds(begin, count)
        return pltpu.make_async_remote_copy(
            src_ref=src.at[rows],
            dst_ref=dst.at[rows],
            send_sem=ring_send.at[i, sem],
            recv_sem=ring_recv.at[i, sem],
            device_id=to,
            device_id_type=MESH,
        )

    def offer_ring(i, quarter):
        piece(i, "up", quarter).start()
        piece(i, "down", quarter).start()

    def spread(i, quarter):
        if i in (UP, DOWN):
            offer_ring(i, quarter)
        piece(i, "core", quarter).start()

    def begin_ring(i):
        piece(i, "send", "left").start()
        piece(i, "send", "right").start()

    def forward_ring(i):
        for quarter in ("left", "right"):
            piece(i, "send", quarter).wait_recv()
            piece(i, "pass", quarter).start()
            spread(i, quarter)

    def share_ring(i):
        piece(i, "pass", "left").wait_recv()
        piece(i, "pass", "right").wait_recv()
        spread(i, "across")

    def swap_ring(i, quarter):
        piece(i, "up", quarter).wait_recv()
        piece(i, "down", quarter).wait_recv()
        piece(i, "swap", quarter).start()

    def finish_ring(i, quarter):
        if quarter == "own":
            local(i).wait()
            return
        piece(i, "core", quarter).wait_recv()
        if i in SWAPPED:
            piece(i, "swap", quarter).wait_recv()

    def drain_ring(i):
        for quarter in ("left", "right", "across"):
            if quarter != "across":
                piece(i, "send", quarter).wait_send()
                piece(i, "pass", quarter).wait_send()
            for kind in ("core",) if i not in SWAPPED else ("up", "down", "core", "swap"):
                piece(i, kind, quarter).wait_send()

    begin_ring(0)
    begin_ring(1)

    recv_in = (recv_in_0, recv_in_1)
    unit_recv = (unit_recv_0, unit_recv_1)
    recv_out = (recv_out_0, recv_out_1)

    def slot(way, send, recv, step, part):
        dest = at(step)
        rows = pl.ds(part * PART, PART)
        return pltpu.make_async_remote_copy(
            src_ref=send.at[dest, rows],
            dst_ref=recv[part].at[me],
            send_sem=a2a_send.at[way, part],
            recv_sem=a2a_recv.at[way, part],
            device_id=(dest, t),
            device_id_type=MESH,
        )

    def send_slots(way, send, recv, part, fill):
        rows = pl.ds(part * PART, PART)
        for step in STEPS:
            send[at(step), rows, :] = fill(at(step), rows)
            slot(way, send, recv, step, part).start()
        recv[part][me] = fill(me, rows)

    def whole(ref, sems, way, part):
        some = ref.at[pl.ds(0, IMG - 1)]
        if ref.shape[1] == ROWS:
            some = ref.at[pl.ds(0, IMG - 1), pl.ds(part * PART, PART)]
        pltpu.make_async_copy(some, some, sems.at[way, part]).wait()

    def image_for(dest, rows):
        return embedded[jnp.maximum(wanted_ref[dest] - 1, 0), rows, :]

    send_slots(0, send_in, recv_in, 0, image_for)
    begin_ring(2)
    begin_ring(3)
    send_slots(0, send_in, recv_in, 1, image_for)
    forward_ring(0)
    forward_ring(1)

    def pair_copy(step, part):
        pair = lax.rem(t + step, TP)
        return pltpu.make_async_remote_copy(
            src_ref=pair_send.at[pair, part],
            dst_ref=pair_recv.at[0, t, part],
            send_sem=pair_sems.at[0, part, 0, step],
            recv_sem=pair_sems.at[0, part, 1, step],
            device_id=(me, pair),
            device_id_type=MESH,
        )

    def pair_pass(step, part):
        quarter = lax.rem(t + TP - step, TP)
        return pltpu.make_async_remote_copy(
            src_ref=pair_recv.at[0, quarter, part],
            dst_ref=pair_recv.at[1, quarter, part],
            send_sem=pair_sems.at[1, part, 0, step],
            recv_sem=pair_sems.at[1, part, 1, step],
            device_id=(taker, t),
            device_id_type=MESH,
        )

    def begin_pairs(part):
        whole(recv_in[part], a2a_recv, 0, part)
        for view in range(VIEWS):
            pair_send[view // 2, part, view % 2] = recv_in[part][mine_ref[view]]
        for step in (2, 1, 3):
            pair_copy(step, part).start()
        pair_recv[0, t, part] = pair_send[t, part]
        pair_pass(0, part).start()

    def pass_pairs(part):
        for step in (1, 3, 2):
            pair_copy(step, part).wait_recv()
            pair_pass(step, part).start()

    def take_unit(unit, part):
        for quarter in range(TP):
            rows = pl.ds(unit * 256 + part * 128 + quarter * PART, PART)
            state[rows, :] = pair_recv[unit, quarter, part, side].astype(jnp.float32)
            partner[rows, :] = pair_recv[unit, quarter, part, 1 - side]
        rows = pl.ds(unit * 256 + part * 128, 128)
        normed[rows, :] = norm(state[rows, :], 0)
        partner[rows, :] = norm(partner[rows, :].astype(jnp.float32), 2)

    def norm(value, which):
        return layer_norm(value, gain_ref[side, pl.ds(which, 1)], bias_ref[side, pl.ds(which, 1)])

    begin_pairs(0)
    share_ring(0)
    share_ring(1)
    forward_ring(2)
    pass_pairs(0)
    take_unit(0, 0)
    forward_ring(3)
    begin_ring(UP)
    share_ring(2)
    begin_pairs(1)
    for quarter in QUARTERS[1:]:
        offer_ring(2, quarter)
    begin_ring(DOWN)
    for step in range(TP):
        pair_pass(step, 0).wait_recv()
    take_unit(1, 0)
    pass_pairs(1)
    share_ring(3)
    take_unit(0, 1)
    forward_ring(UP)

    for i in range(2):
        for quarter in QUARTERS:
            finish_ring(i, quarter)

    def heads(q, k, v):
        def cut(value, unit, head):
            return value[unit * 256 : unit * 256 + 256, head * HEAD : head * HEAD + HEAD]

        found = attend([[cut(x, unit, head) for x in (q, k, v)] for unit in range(q.shape[0] // 256) for head in range(3)])
        return [jnp.concatenate(found[n : n + 3], axis=1) for n in range(0, len(found), 3)]

    def self_group(unit, group, carry):
        if unit == 0:

            @pl.when(group == 3)
            def _():
                swap_ring(2, "right")
                swap_ring(2, "left")
                swap_ring(2, "across")

        else:

            @pl.when(group == 1)
            def _():
                share_ring(UP)
                forward_ring(DOWN)

            @pl.when(group == 3)
            def _():
                swap_ring(UP, "left")
                swap_ring(UP, "right")

        rows = pl.ds(unit * 256, 256)
        qkv = dot_t(normed[rows, :], w_self[group]).astype(jnp.bfloat16)
        found = heads(qkv[:, 0:192], qkv[:, 192:384], qkv[:, 384:576])
        state[rows, :] += dot(found[0], w_so[group])
        return carry

    lax.fori_loop(0, TP, functools.partial(self_group, 0), 0)
    for step in range(TP):
        pair_pass(step, 1).wait_recv()
    take_unit(1, 1)
    lax.fori_loop(0, TP, functools.partial(self_group, 1), 0)

    for unit in range(2):
        rows = pl.ds(unit * 256, 256)
        normed[rows, :] = norm(state[rows, :], 1)
    finish_ring(2, "own")
    finish_ring(3, "own")

    def cross_group(i, carry):
        @pl.when(i == 0)
        def _():
            share_ring(DOWN)

        @pl.when(i == 2)
        def _():
            swap_ring(UP, "across")

        @pl.when(i == 3)
        def _():
            swap_ring(DOWN, "right")
            swap_ring(DOWN, "left")

        for n in range(1, TP):

            @pl.when(i == n)
            def _():
                finish_ring(2, QUARTERS[n])
                finish_ring(3, QUARTERS[n])

        group = lax.rem(t + i * (i + 1) // 2, TP)
        q = dot_t(normed[...], w_cross[group, 0:192]).astype(jnp.bfloat16)
        kv = dot_t(partner[...], w_cross[group, 192:576]).astype(jnp.bfloat16)
        found = heads(q, kv[:, 0:192], kv[:, 192:384])
        state[...] += dot(jnp.concatenate(found, axis=0), w_co[group])
        return carry

    lax.fori_loop(0, TP, cross_group, 0)

    for unit in range(2):
        rows = pl.ds(unit * 256, 256)
        normed[rows, :] = norm(state[rows, :], 3)

    def mlp(value, group):
        hidden = dot(value, w_up[group])
        hidden = hidden * (lax.erf(hidden * 0.5**0.5) + 1.0) * 0.5
        return dot(hidden.astype(jnp.bfloat16), w_down[group])

    finish_ring(UP, "own")
    finish_ring(DOWN, "own")

    def mlp_group(i, carry):
        @pl.when(i == 1)
        def _():
            swap_ring(DOWN, "across")
            finish_ring(UP, "right")
            finish_ring(DOWN, "right")

        @pl.when(i == 2)
        def _():
            finish_ring(UP, "left")
            finish_ring(DOWN, "left")

        state[...] += mlp(normed[...], lax.rem(t + i * (i + 1) // 2, TP))
        return carry

    lax.fori_loop(0, TP - 1, mlp_group, 0)
    finish_ring(UP, "across")
    finish_ring(DOWN, "across")

    def unit_copy(unit, step, part):
        quarter = lax.rem(t + step, TP)
        rows = pl.ds(part * PART, PART)
        return pltpu.make_async_remote_copy(
            src_ref=unit_send.at[unit, quarter, rows],
            dst_ref=unit_recv[part].at[t, side],
            send_sem=pair_sems.at[2 + unit, part, 0, step],
            recv_sem=pair_sems.at[2 + unit, part, 1, step],
            device_id=((me, giver)[unit], quarter),
            device_id_type=MESH,
        )

    others = [(unit, step) for step in (2, 1, 3, 0) for unit in (1, 0) if unit or step]

    def last_group(part, carry):
        picks = [pl.ds(pl.multiple_of(unit * 256 + part * 128, 128), 128) for unit in range(2)]
        done = mlp(jnp.concatenate([normed[rows, :] for rows in picks], axis=0), across)
        for unit in range(2):
            value = state[picks[unit], :] + done[unit * 128 : unit * 128 + 128]
            for quarter in range(TP):
                unit_send[unit, quarter, pl.ds(pl.multiple_of(part * PART, PART), PART), :] = value[
                    quarter * PART : quarter * PART + PART
                ].astype(jnp.bfloat16)
        return carry

    def begin_units(part):
        for unit, step in others:
            unit_copy(unit, step, part).start()
        rows = pl.ds(part * PART, PART)
        unit_recv[part][t, side] = unit_send[0, t, rows, :]

    def begin_return(part):
        for unit, step in others:
            unit_copy(unit, step, part).wait_recv()
        def view_for(dest, rows):
            view = back_ref[dest]
            return unit_recv[part][view // 2, lax.rem(view, 2)]

        send_slots(1, send_out, recv_out, part, view_for)

    last_group(0, 0)
    begin_units(0)
    last_group(1, 0)
    begin_units(1)
    begin_return(0)
    begin_return(1)

    for i in range(len(SHARE)):
        drain_ring(i)
    for part in range(2):
        for step in range(TP):
            if step:
                pair_copy(step, part).wait_send()
            pair_pass(step, part).wait_send()
        for unit, step in others:
            unit_copy(unit, step, part).wait_send()
        whole(send_in, a2a_send, 0, part)

    def add_rows(part, chunk, carry):
        rows = pl.ds(pl.multiple_of(chunk * 16, 16), 16)
        sums = [jnp.zeros((16, D), jnp.float32) for _ in range(4)]
        for worker in range(IMG):
            value = recv_out[part][worker, rows, :].astype(jnp.float32)
            image_here = wanted_ref[worker] - 1
            for image in range(4):
                sums[image] += jnp.where(image_here == image, value, 0.0)
        for image in range(4):
            out_ref[image, pl.ds(pl.multiple_of(part * PART + chunk * 16, 16), 16), :] = sums[image].astype(jnp.bfloat16)
        return carry

    for part in range(2):
        whole(recv_out[part], a2a_recv, 1, part)
        lax.fori_loop(0, 2, functools.partial(add_rows, part), 0)
    for part in range(2):
        whole(send_out, a2a_send, 1, part)


def per_device(
    tokens,
    image_pairs,
    image_row,
    embed_weight,
    norm_gain,
    norm_bias,
    self_qkv,
    self_out,
    cross_qkv,
    cross_out,
    mlp_up,
    mlp_down,
):
    img_dev = tokens.shape[0]
    bf16 = jnp.bfloat16
    smem = pl.BlockSpec(memory_space=pltpu.SMEM)
    vmem = pl.BlockSpec(memory_space=pltpu.VMEM)
    hbm = pl.BlockSpec(memory_space=pl.ANY)
    return pl.pallas_call(
        kernel,
        out_shape=jax.ShapeDtypeStruct((img_dev, ROWS, D), bf16),
        in_specs=[smem] * 2 + [vmem] * 4 + [hbm] * 6,
        out_specs=vmem,
        scratch_shapes=[
            *(pltpu.VMEM((TP, rows, D), bf16) for rows in SHARE),
            pltpu.VMEM((4, ROWS, D), bf16),
            pltpu.VMEM((IMG, ROWS, D), bf16),
            pltpu.VMEM((IMG, PART, D), bf16),
            pltpu.VMEM((IMG, PART, D), bf16),
            pltpu.VMEM((4, 2, 2, PART, D), bf16),
            pltpu.VMEM((2, TP, 2, 2, PART, D), bf16),
            pltpu.VMEM((512, D), jnp.float32),
            pltpu.VMEM((512, D), bf16),
            pltpu.VMEM((512, D), bf16),
            pltpu.VMEM((2, TP, ROWS, D), bf16),
            pltpu.VMEM((4, 2, PART, D), bf16),
            pltpu.VMEM((4, 2, PART, D), bf16),
            pltpu.VMEM((IMG, ROWS, D), bf16),
            pltpu.VMEM((IMG, PART, D), bf16),
            pltpu.VMEM((IMG, PART, D), bf16),
            pltpu.SMEM((IMG,), jnp.int32),
            pltpu.SMEM((VIEWS,), jnp.int32),
            pltpu.SMEM((IMG,), jnp.int32),
            pltpu.SemaphoreType.DMA((len(SHARE),)),
            pltpu.SemaphoreType.DMA((len(SHARE), 16)),
            pltpu.SemaphoreType.DMA((len(SHARE), 16)),
            pltpu.SemaphoreType.DMA((2, 2)),
            pltpu.SemaphoreType.DMA((2, 2)),
            pltpu.SemaphoreType.DMA((4, 2, 2, TP)),
        ],
        compiler_params=pltpu.CompilerParams(
            collective_id=0, has_side_effects=True, vmem_limit_bytes=60 * 1024 * 1024
        ),
    )(
        image_pairs.T,
        image_row,
        tokens,
        embed_weight,
        norm_gain,
        norm_bias,
        jnp.swapaxes(self_qkv, 2, 3).reshape(2, 576, D),
        jnp.swapaxes(cross_qkv, 2, 3).reshape(2, 576, D),
        self_out,
        cross_out,
        mlp_up,
        mlp_down,
    )


def solution(mesh):
    in_specs = (
        P("img", "tp", None),
        P(),
        P(),
        P(),
        P(),
        P(),
        P(None, None, None, "tp"),
        P(None, "tp", None),
        P(None, None, None, "tp"),
        P(None, "tp", None),
        P(None, None, "tp"),
        P(None, "tp", None),
    )
    out_specs = P("img", "tp", None)
    return jax.shard_map(
        per_device, mesh=mesh, in_specs=in_specs, out_specs=out_specs, check_vma=False
    )
```
